512 devices in a mesh: dp: 4 (over x), ctx: 16 (over y_lo, z), vocab: 8 (over y_hi, core).
Axes of the slice: x: 4, y: 8 (y_hi: 4, y_lo: 2; y = y_hi * 2 + y_lo), z: 8, core: 2. Of those that a mesh axis runs over, the one named last changes fastest.
Arguments:
- hidden: bfloat16 [32768, 5376], P(('dp', 'ctx'), 'vocab'), may hold values from -60 to 60
- embedding: bfloat16 [1024, 5376], P('vocab', ('dp', 'ctx')), may hold values from -1 to 1, as said below
- targets: int32 [32768], P(('dp', 'ctx')), may hold values from 0 to 1023, as said below
- pattern: int32 [256, 8], P(('dp', 'ctx'), 'vocab'), may hold values from 0 to 1, as said below
- loss_grad: float32 [32768], P(('dp', 'ctx')), may hold values from 0.3 to 3
Outputs:
- loss: float32 [32768], P(('dp', 'ctx'))
- hidden_grad: bfloat16 [32768, 5376], P(('dp', 'ctx'), 'vocab')
- embedding_grad: float32 [1024, 5376], P('vocab', ('dp', 'ctx'))
The draws below stay inside these ranges and needn't reach their ends.
Inputs may be any that keep to these rules, and one draw needn't show every extreme that they name: `targets`: each token's target lies in a vocabulary block that pattern marks for the token's block. `pattern`: every token block has at least one marked vocabulary block. `embedding`: every row has unit Euclidean length before rounding.
All inputs are finite; a program needn't handle non-finite values.
Results may differ from the reference program's by a relative error of at most 0.005.
Values may be sent and summed in bfloat16 or wider, within the bound.
A program may use at most 64 MiB of HBM per device.

```python
import math
import jax
import jax.numpy as jnp
from jax import lax

D = 5376
TILE = 128
VOCAB = 1024
TOKENS = 32768


def block_pattern(key):
    base = jax.random.fold_in(key, 101)
    keys = jax.random.split(base, 5)
    token_blocks = TOKENS // TILE
    vocab_blocks = VOCAB // TILE
    thresh = jax.random.randint(keys[0], (1, vocab_blocks), 10, 90)
    roll = jax.random.randint(keys[1], (token_blocks, vocab_blocks), 0, 100)
    forced = jax.random.randint(keys[2], (token_blocks,), 0, vocab_blocks)
    block_ids = jnp.arange(vocab_blocks, dtype=jnp.int32)
    marks = jnp.logical_or(roll < thresh, block_ids[None, :] == forced[:, None]).astype(jnp.int32)
    counts = jnp.sum(marks, axis=1)
    row_marks = jnp.repeat(marks, TILE, axis=0)
    row_counts = jnp.repeat(counts, TILE)
    picks = jax.random.randint(keys[3], (TOKENS,), 0, 1 << 20) % row_counts
    ranks = jnp.cumsum(row_marks, axis=1) - 1
    chosen_mask = jnp.logical_and(row_marks > 0, ranks == picks[:, None])
    chosen = jnp.sum(jnp.where(chosen_mask, block_ids[None, :], 0), axis=1)
    inner = jax.random.randint(keys[4], (TOKENS,), 0, TILE)
    targets = (chosen * TILE + inner).astype(jnp.int32)
    return (marks, targets)


def embed_table(key):
    base = jax.random.fold_in(key, 202)
    table = jnp.clip(jax.random.normal(base, (VOCAB, D), jnp.float32), -6.0, 6.0)
    return table / jnp.sqrt(jnp.sum(table * table, axis=1, keepdims=True))


def draw_embedding(key, part):
    table = embed_table(key)
    return table.astype(jnp.bfloat16)


def draw_targets(key, part):
    marks, targets = block_pattern(key)
    return targets


def draw_pattern(key, part):
    marks, targets = block_pattern(key)
    return marks


def draw_hidden(key, part):
    key = jax.random.fold_in(key, 5)
    first_key = jax.random.fold_in(key, 0)
    values = 3.0 * jnp.clip(jax.random.normal(first_key, (TOKENS, D), jnp.float32), -6.0, 6.0)
    return jnp.clip(values, -60.0, 60.0).astype(jnp.bfloat16)


def block_levels(key, extent, pieces, least, high):
    gain, own = 1.0, jax.random.fold_in(key, 6)
    for axis_at, blocks in pieces:
        draws = jnp.exp(jax.random.uniform(jax.random.fold_in(own, axis_at), (blocks,), jnp.float32, least / len(pieces), high / len(pieces)))
        gain = gain * jnp.repeat(draws, extent[axis_at] // blocks).reshape([-1 if axis == axis_at else 1 for axis in range(len(extent))])
    return gain


def setup_inputs(seed: int = 0) -> dict:
    splits = jax.random.split(jax.random.key(seed), 6)
    return {
        "hidden": draw_hidden(jax.random.fold_in(splits[5], 71), 0),
        "embedding": draw_embedding(jax.random.fold_in(splits[5], 71), 0),
        "targets": draw_targets(jax.random.fold_in(splits[5], 71), 0),
        "pattern": draw_pattern(jax.random.fold_in(splits[5], 71), 0),
        "loss_grad": jnp.clip(jnp.exp(math.log(3.0) - 2.3025851 * jax.random.uniform(splits[4], (TOKENS,), jnp.float32) ** block_levels(splits[4], (TOKENS,), ((0, 64),), -0.2, 0.2)), 0.3, 3.0),
    }


def reference(hidden, embedding, targets, pattern, loss_grad):
    logits = lax.dot_general(hidden, embedding, (((1,), (1,)), ((), ())), preferred_element_type=jnp.float32)
    live = jnp.repeat(jnp.repeat(pattern > 0, TILE, axis=0), TILE, axis=1)
    peak = jnp.max(jnp.where(live, logits, jnp.float32(-1e30)), axis=1)
    total = jnp.sum(jnp.where(live, jnp.exp(logits - peak[:, None]), jnp.float32(0.0)), axis=1)
    lse = peak + jnp.log(total)
    target_logit = jnp.take_along_axis(logits, targets[:, None].astype(jnp.int32), axis=1)[:, 0]
    loss = lse - target_logit
    columns = lax.iota(jnp.int32, VOCAB)
    target_hit = (targets[:, None] == columns[None, :]).astype(jnp.float32)
    probs = jnp.where(live, jnp.exp(logits - lse[:, None]), jnp.float32(0.0))
    logit_grad = (loss_grad[:, None] * (probs - target_hit)).astype(jnp.bfloat16)
    hidden_grad = jnp.dot(logit_grad, embedding, preferred_element_type=jnp.float32).astype(jnp.bfloat16)
    embedding_grad = lax.dot_general(logit_grad, hidden, (((0,), (0,)), ((), ())), preferred_element_type=jnp.float32)
    return (loss, hidden_grad, embedding_grad)
```

```python
import jax
import jax.numpy as jnp
from jax import lax
from jax.experimental import pallas as pl
from jax.experimental.pallas import tpu as pltpu
from jax.sharding import PartitionSpec as P

MESH = pl.DeviceIdType.MESH
BF = jnp.bfloat16
F32 = jnp.float32
DEAD = -1e30
NX, NL, NZ, NH, NC = 4, 2, 8, 4, 2
TILE = 128
HALF = 64
TOK = 512
FEAT = 672
PIECE = 84
PAD = 96
HROW = FEAT // 2
NSEM = 128


def nt(a, b):
    return lax.dot_general(a, b, (((1,), (1,)), ((), ())), preferred_element_type=F32)


def nn(a, b):
    return jnp.dot(a, b, preferred_element_type=F32)


def iotas(shape):
    return lax.broadcasted_iota(jnp.int32, shape, 0), lax.broadcasted_iota(jnp.int32, shape, 1)


def mask_bf16(cond):
    return jnp.where(cond, 1.0, 0.0).astype(BF)


def kernel(
    hid, emb, tgt, pat, lgr, loss_o, hg_o, eg_o,
    piece, stage, sel, selt, hidt, et, sbuf, sib, opp, opp_a, opp_b, nbr_p, nbr_m, in_p, in_m, lsum,
    gbuf, lbuf, xo, xs, xin, tbuf, pieces, pin, ssem, rsem,
):
    x = lax.axis_index("dp")
    ctx = lax.axis_index("ctx")
    v = lax.axis_index("vocab")
    l, z = lax.div(ctx, NZ), lax.rem(ctx, NZ)
    h, c = lax.div(v, NC), lax.rem(v, NC)

    def dev(x, l, z, h, c):
        return (x, l * NZ + z, h * NC + c)

    def add(a, d, n):
        return lax.rem(a + d, n)

    sibling = dev(x, l, z, h, 1 - c)
    hp, hm = dev(x, l, z, add(h, 1, NH), c), dev(x, l, z, add(h, 3, NH), c)
    xp, xm = dev(add(x, 1, NX), l, z, h, c), dev(add(x, 3, NX), l, z, h, c)
    yl = dev(x, 1 - l, z, h, c)
    diag = jnp.logical_and(x == h, l == c)
    off_diag = jnp.logical_not(diag)

    bar = pltpu.get_barrier_semaphore()

    def greet(who):
        pl.semaphore_signal(bar, inc=1, device_id=who, device_id_type=MESH)

    others = [(dq, dc) for dq in range(NH) for dc in range(NC) if dq or dc]
    others_dev = [dev(x, l, z, add(h, dq, NH), add(c, dc, NC)) for dq, dc in others]
    turned = [dev(h, c, add(z, d, NZ), x, l) for d in range(NZ)]
    away = [dev(h, c, add(z, d, NZ), x, 1 - l) for d in range(NZ)]
    away_src = [dev(h, 1 - c, add(z, d, NZ), x, l) for d in range(NZ)]
    for who in others_dev + [xp, xm, yl] + turned[1:] + away_src:
        greet(who)

    @pl.when(off_diag)
    def _():
        greet(turned[0])

    count = [0]
    sent = []

    def copy(src, dst, to):
        i = count[0]
        count[0] += 1
        return pltpu.make_async_remote_copy(
            src_ref=src, dst_ref=dst, send_sem=ssem.at[i], recv_sem=rsem.at[i],
            device_id=to, device_id_type=MESH,
        )

    def send(src, dst, to):
        cp = copy(src, dst, to)
        cp.start()
        sent.append(cp)
        return cp

    a, b = iotas((PAD, PIECE))
    piece[...] = nt(mask_bf16(a == b), emb[...]).astype(BF)

    peers = len(others) + 3 + (NZ - 1) + NZ
    pl.semaphore_wait(bar, jnp.where(off_diag, peers + 1, peers))

    first = [copy(piece, stage.at[z], turned[0])]

    @pl.when(off_diag)
    def _():
        first[0].start()

    for d in range(1, NZ):
        first.append(send(piece, stage.at[z], turned[d]))

    @pl.when(diag)
    def _():
        stage[z] = piece[...]

    a, b = iotas((FEAT, NZ * PAD))
    q = (b * 683) >> 16
    sel[...] = mask_bf16(jnp.logical_and(b - PAD * q < PIECE, a == b - (PAD - PIECE) * q))
    b, a = iotas((NZ * PAD, FEAT))
    q = (b * 683) >> 16
    selt[...] = mask_bf16(jnp.logical_and(b - PAD * q < PIECE, a == b - (PAD - PIECE) * q))
    a, b = iotas((FEAT, FEAT))
    hidt[...] = nt(mask_bf16(a == b), hid[...]).astype(BF)

    @pl.when(off_diag)
    def _():
        first[0].wait()

    for cp in first[1:]:
        cp.wait_recv()
    et[0] = nn(sel[...], stage[...].reshape(NZ * PAD, TILE)).astype(BF)

    rows2 = [pl.ds(0, HROW), pl.ds(HROW, HROW)]

    def pass_on(src, dst, to, half):
        return send(et.at[src, rows2[half]], et.at[dst, rows2[half]], to)

    a1, a2, a3, b2, b3, c2, c3 = [], [], [], [], [], [], []
    for half in range(2):
        a1.append(pass_on(0, 1, yl, half))
        a2.append(pass_on(0, 6, xp, half))
        a3.append(pass_on(0, 2, xm, half))
    for half in range(2):
        a1[half].wait_recv()
        b2.append(pass_on(1, 7, xp, half))
        b3.append(pass_on(1, 3, xm, half))
        a3[half].wait_recv()
        c3.append(pass_on(2, 4, xm, half))

    sib_cp, opp_cp, nbr_cp = {}, {}, {}

    def weights(r):
        return jnp.concatenate([et[2 * r], et[2 * r + 1]], axis=1)

    def logits(r):
        s = nn(hid[...], weights(r))
        base = lax.rem(x + r, NX) * 2
        _, lane = iotas((TILE, 2 * TILE))
        block = base + jnp.where(lane < TILE, l, 1 - l)
        for t in range(NH):
            off = jnp.logical_and(block == v, pat[t : t + 1, 0:1] == 0)
            part = jnp.where(off, DEAD, s[t * TILE : (t + 1) * TILE])
            sbuf[r, t] = part.reshape(NC, HALF, 2 * TILE)
        sib_cp[r] = send(sbuf.at[r, :, 1 - c], sib.at[r], sibling)

    def mine(r, dq, rows=slice(None)):
        t = add(h, dq, NH)
        return sbuf[r, t, c, rows] + sib[r, t, rows]

    lo, hi = pl.ds(0, HALF // 2), pl.ds(HALF // 2, HALF // 2)

    def to_far(r):
        sib_cp[r].wait_recv()
        opp[r] = mine(r, 2)
        opp_cp[r] = (
            send(opp.at[r, lo], opp_a.at[r], hp),
            send(opp.at[r, hi], opp_b.at[r], hm),
        )

    def to_near(r):
        near_p, near_m = mine(r, 1), mine(r, 3)
        opp_cp[r][0].wait_recv()
        nbr_p[r] = jnp.concatenate([near_p[: HALF // 2] + opp_a[r], near_p[HALF // 2 :]], axis=0)
        p = send(nbr_p.at[r], in_p.at[r], hp)
        opp_cp[r][1].wait_recv()
        nbr_m[r] = jnp.concatenate([near_m[: HALF // 2], near_m[HALF // 2 :] + opp_b[r]], axis=0)
        nbr_cp[r] = (p, send(nbr_m.at[r], in_m.at[r], hm))

    def whole(r):
        own = mine(r, 0)
        nbr_cp[r][0].wait_recv()
        nbr_cp[r][1].wait_recv()
        lsum[r] = own + in_p[r] + in_m[r]

    logits(0)
    b2[0].wait_recv()
    c2.append(pass_on(7, 5, xp, 0))
    to_far(0)
    b2[1].wait_recv()
    c2.append(pass_on(7, 5, xp, 1))
    for cp in b3:
        cp.wait_recv()
    logits(1)
    for cp in a2:
        cp.wait_recv()
    logits(3)
    to_near(0)
    to_far(1)
    to_far(3)
    to_near(1)
    to_near(3)
    for cp in c3 + c2:
        cp.wait_recv()
    logits(2)
    to_far(2)
    whole(0)
    whole(1)
    whole(3)
    to_near(2)
    whole(2)

    sub, lane = iotas((HALF, TILE))
    turn = sub + c * HALF == lane

    def column(row):
        return jnp.sum(jnp.where(turn, row, 0.0), axis=1, keepdims=True)

    target = column(tgt[pl.ds(h, 1), :].astype(F32)).astype(jnp.int32)
    scale = column(lgr[pl.ds(h, 1), :])
    _, lane2 = iotas((HALF, 2 * TILE))
    hits, ls = [], []
    for r in range(NX):
        col = lax.rem(x + r, NX) * 2 * TILE + jnp.where(lane2 < TILE, l, 1 - l) * TILE
        hits.append(col + jnp.where(lane2 < TILE, lane2, lane2 - TILE) == target)
        ls.append(lsum[r])
    peak = jnp.max(jnp.maximum(jnp.maximum(ls[0], ls[1]), jnp.maximum(ls[2], ls[3])), axis=1, keepdims=True)
    total = sum(jnp.exp(s - peak) for s in ls)
    total = jnp.sum(total, axis=1, keepdims=True)
    lse = peak + jnp.log(total)
    at_target = sum(jnp.where(hit, s, 0.0) for hit, s in zip(hits, ls))
    loss = lse - jnp.sum(at_target, axis=1, keepdims=True)
    own_rows = pl.ds(pl.multiple_of(h * TILE + c * HALF, HALF), HALF)
    order = (2, 1, 3, 0)
    g_sib, g_p, g_m, f_p, f_m, relay = {}, {}, {}, {}, {}, {}
    for r in order:
        probs = jnp.exp(ls[r] - lse)
        gbuf[r, own_rows] = (scale * (probs - jnp.where(hits[r], 1.0, 0.0))).astype(BF)
        mine_g = gbuf.at[r, own_rows]
        g_p[r] = send(mine_g, mine_g, hp)
        g_m[r] = send(mine_g, mine_g, hm)
        g_sib[r] = send(mine_g, mine_g, sibling)
    loss_row = jnp.sum(jnp.where(turn, loss, 0.0), axis=0, keepdims=True)
    lbuf[v] = jnp.broadcast_to(loss_row, (8, TILE))
    loss_cp = [send(lbuf.at[v], lbuf.at[v], who) for who in others_dev]

    def rows_of(dq, start, size):
        return pl.ds(pl.multiple_of(add(h, dq, NH) * TILE + c * HALF + start, size), size)

    def forward(r):
        g_p[r].wait_recv()
        near_m = gbuf.at[r, rows_of(3, HALF // 2, HALF // 2)]
        f_p[r] = send(near_m, near_m, hp)
        g_m[r].wait_recv()
        near_p = gbuf.at[r, rows_of(1, 0, HALF // 2)]
        f_m[r] = send(near_p, near_p, hm)
        relay[r] = []
        for dq in (3, 1):
            part = gbuf.at[r, rows_of(dq, 0, HALF)]
            relay[r].append(send(part, part, sibling))

    def forward_far(r):
        f_p[r].wait_recv()
        f_m[r].wait_recv()
        part = gbuf.at[r, rows_of(2, 0, HALF)]
        relay[r].append(send(part, part, sibling))

    def gathered(r):
        g_sib[r].wait_recv()
        for cp in relay[r]:
            cp.wait_recv()

    def grad(r):
        return nn(hidt[...], gbuf[r])

    x_cp = {}
    forward(2)
    forward(1)
    forward_far(2)
    gathered(2)
    d = grad(2)
    xo[0] = d[:, :TILE].astype(BF)
    x_cp["far_p"] = send(xo.at[0], xin.at[0], xp)
    xo[1] = d[:, TILE:].astype(BF)
    x_cp["far_m"] = send(xo.at[1], xin.at[1], xm)
    forward(3)
    forward_far(1)
    gathered(1)
    d = grad(1)
    xo[2] = d[:, TILE:].astype(BF)
    x_cp["p1"] = send(xo.at[2], xin.at[2], xp)
    tbuf[0] = d[:, :TILE]
    forward(0)
    forward_far(3)
    gathered(3)
    d = grad(3)
    xo[3] = d[:, :TILE].astype(BF)
    x_cp["m0"] = send(xo.at[3], xin.at[3], xm)
    tbuf[1] = d[:, TILE:]
    x_cp["far_p"].wait_recv()
    xs[0] = (tbuf[0] + xin[0].astype(F32)).astype(BF)
    x_cp["p0"] = send(xs.at[0], xin.at[4], xp)
    x_cp["far_m"].wait_recv()
    xs[1] = (tbuf[1] + xin[1].astype(F32)).astype(BF)
    x_cp["m1"] = send(xs.at[1], xin.at[5], xm)
    forward_far(0)
    gathered(0)
    d = grad(0)
    tbuf[0] = d[:, :TILE]
    tbuf[1] = d[:, TILE:]

    hg = nt(gbuf[0], weights(0))
    for r in range(1, NX):
        hg = hg + nt(gbuf[r], weights(r))
    hg_o[...] = hg.astype(BF)
    for cp in loss_cp:
        cp.wait_recv()
    for t in range(NH):
        loss_o[t : t + 1, :] = lbuf[2 * t, 0:1, :] + lbuf[2 * t + 1, 0:1, :]

    last = [[], []]
    for m, (near, far) in enumerate(((4, 3), (2, 5))):
        x_cp[("p0", "p1")[m]].wait_recv()
        x_cp[("m0", "m1")[m]].wait_recv()
        tot = tbuf[m] + xin[near].astype(F32) + xin[far].astype(F32)
        pieces[m] = nn(selt[...], tot.astype(BF)).astype(BF).reshape(NZ, PAD, TILE)
        for d in range(NZ):
            cp = copy(pieces.at[m, add(z, d, NZ)], pin.at[m, z], (turned, away)[m][d])
            last[m].append(cp)
            if d or m:
                cp.start()
                sent.append(cp)

    @pl.when(off_diag)
    def _():
        last[0][0].start()

    @pl.when(diag)
    def _():
        pin[0, z] = pieces[0, z]

    for cp in last[0][1:] + last[1]:
        cp.wait_recv()

    @pl.when(off_diag)
    def _():
        last[0][0].wait()

    acc = None
    for m in range(2):
        for zz in range(NZ):
            p = pin[m, zz].astype(F32)
            acc = p if acc is None else acc + p
    full = jnp.concatenate([acc, jnp.zeros((TILE - PAD, TILE), F32)], axis=0)
    eg_o[...] = full.T[:, :PIECE]
    for cp in sent:
        cp.wait_send()


def on_device(hidden, embedding, targets, pattern, loss_grad):
    vmem = pl.BlockSpec(memory_space=pltpu.VMEM)
    loss, hidden_grad, embedding_grad = pl.pallas_call(
        kernel,
        out_shape=(
            jax.ShapeDtypeStruct((NH, TILE), F32),
            jax.ShapeDtypeStruct((TOK, FEAT), BF),
            jax.ShapeDtypeStruct((TILE, PIECE), F32),
        ),
        in_specs=[vmem] * 5,
        out_specs=(vmem,) * 3,
        scratch_shapes=[
            pltpu.VMEM((PAD, TILE), BF),
            pltpu.VMEM((NZ, PAD, TILE), BF),
            pltpu.VMEM((FEAT, NZ * PAD), BF),
            pltpu.VMEM((NZ * PAD, FEAT), BF),
            pltpu.VMEM((FEAT, TOK), BF),
            pltpu.VMEM((8, FEAT, TILE), BF),
            pltpu.VMEM((NX, NH, NC, HALF, 2 * TILE), F32),
            pltpu.VMEM((NX, NH, HALF, 2 * TILE), F32),
            pltpu.VMEM((NX, HALF, 2 * TILE), F32),
            pltpu.VMEM((NX, HALF // 2, 2 * TILE), F32),
            pltpu.VMEM((NX, HALF // 2, 2 * TILE), F32),
            pltpu.VMEM((NX, HALF, 2 * TILE), F32),
            pltpu.VMEM((NX, HALF, 2 * TILE), F32),
            pltpu.VMEM((NX, HALF, 2 * TILE), F32),
            pltpu.VMEM((NX, HALF, 2 * TILE), F32),
            pltpu.VMEM((NX, HALF, 2 * TILE), F32),
            pltpu.VMEM((NX, TOK, 2 * TILE), BF),
            pltpu.VMEM((NH * NC, 8, TILE), F32),
            pltpu.VMEM((4, FEAT, TILE), BF),
            pltpu.VMEM((2, FEAT, TILE), BF),
            pltpu.VMEM((6, FEAT, TILE), BF),
            pltpu.VMEM((2, FEAT, TILE), F32),
            pltpu.VMEM((2, NZ, PAD, TILE), BF),
            pltpu.VMEM((2, NZ, PAD, TILE), BF),
            pltpu.SemaphoreType.DMA((NSEM,)),
            pltpu.SemaphoreType.DMA((NSEM,)),
        ],
        compiler_params=pltpu.CompilerParams(
            collective_id=0, has_side_effects=True, vmem_limit_bytes=48 << 20
        ),
    )(hidden, embedding, targets.reshape(NH, TILE), pattern, loss_grad.reshape(NH, TILE))
    return loss.reshape(TOK), hidden_grad, embedding_grad


def solution(mesh):
    return jax.shard_map(
        on_device,
        mesh=mesh,
        in_specs=(
            P(("dp", "ctx"), "vocab"),
            P("vocab", ("dp", "ctx")),
            P(("dp", "ctx")),
            P(("dp", "ctx"), "vocab"),
            P(("dp", "ctx")),
        ),
        out_specs=(P(("dp", "ctx")), P(("dp", "ctx"), "vocab"), P("vocab", ("dp", "ctx"))),
        check_vma=False,
    )
```

```python
import jax
import jax.numpy as jnp
from jax import lax
from jax.experimental import pallas as pl
from jax.experimental.pallas import tpu as pltpu
from jax.sharding import PartitionSpec as P

MESH = pl.DeviceIdType.MESH
BF = jnp.bfloat16
F32 = jnp.float32
I16 = jnp.int16
DEAD = -1e30
TOP = 32767.0
NX, NL, NZ, NH, NC = 4, 2, 8, 4, 2
TILE = 128
HALF = 64
WIDE = 2 * TILE
TOK = 512
FEAT = 672
PIECE = 84
PAD = 96
HROW = FEAT // 2
NSEM = 128


def nt(a, b):
    return lax.dot_general(a, b, (((1,), (1,)), ((), ())), preferred_element_type=F32)


def nn(a, b):
    return jnp.dot(a, b, preferred_element_type=F32)


def iotas(shape):
    return lax.broadcasted_iota(jnp.int32, shape, 0), lax.broadcasted_iota(jnp.int32, shape, 1)


def mask_bf16(cond):
    return jnp.where(cond, 1.0, 0.0).astype(BF)


def largest(a):
    return jnp.max(jnp.max(a, axis=1, keepdims=True), axis=0, keepdims=True)


def kernel(
    hidt, embt, tgt, pat, lgr, loss_o, hg_o, eg_o,
    piece, stage, sel, selt, hid, et, sbuf, sib, qout, qstep, qin, qin_step, lsum,
    gbuf, lbuf, xo, xs, xin, tbuf, pieces, pin, zsum, fin, ssem, rsem,
):
    x = lax.axis_index("dp")
    ctx = lax.axis_index("ctx")
    v = lax.axis_index("vocab")
    l, z = lax.div(ctx, NZ), lax.rem(ctx, NZ)
    h, c = lax.div(v, NC), lax.rem(v, NC)

    def dev(x, l, z, h, c):
        return (x, l * NZ + z, h * NC + c)

    def add(a, d, n):
        return lax.rem(a + d, n)

    sibling = dev(x, l, z, h, 1 - c)
    ring_h = [dev(x, l, z, add(h, dq, NH), c) for dq in range(NH)]
    xp, xm = dev(add(x, 1, NX), l, z, h, c), dev(add(x, 3, NX), l, z, h, c)
    yl = dev(x, 1 - l, z, h, c)
    ring_z = [dev(x, l, add(z, d, NZ), h, c) for d in range(NZ)]
    turned = dev(h, c, z, x, l)
    away, away_src = dev(h, c, z, x, 1 - l), dev(h, 1 - c, z, x, l)
    diag = jnp.logical_and(x == h, l == c)
    off_diag = jnp.logical_not(diag)

    bar = pltpu.get_barrier_semaphore()

    def greet(who):
        pl.semaphore_signal(bar, inc=1, device_id=who, device_id_type=MESH)

    others = [(dq, dc) for dq in range(NH) for dc in range(NC) if dq or dc]
    others_dev = [dev(x, l, z, add(h, dq, NH), add(c, dc, NC)) for dq, dc in others]
    met = others_dev + [xp, xm, yl] + ring_z[1:] + [away_src]

    @pl.when(off_diag)
    def _():
        greet(turned)

    for who in met:
        greet(who)

    count = [0]
    sent = []

    def copy(src, dst, to):
        i = count[0]
        count[0] += 1
        cp = pltpu.make_async_remote_copy(
            src_ref=src, dst_ref=dst, send_sem=ssem.at[i], recv_sem=rsem.at[i],
            device_id=to, device_id_type=MESH,
        )
        return cp

    def send(src, dst, to):
        cp = copy(src, dst, to)
        cp.start()
        sent.append(cp)
        return cp

    piece[...] = jnp.zeros((PAD, TILE), BF)
    piece[:PIECE] = embt[...]
    pl.semaphore_wait(bar, jnp.where(off_diag, len(met) + 1, len(met)))
    swap = copy(piece, stage.at[z], turned)

    @pl.when(off_diag)
    def _():
        swap.start()

    @pl.when(diag)
    def _():
        stage[z] = piece[...]

    a, b = iotas((FEAT, NZ * PAD))
    q = (b * 683) >> 16
    sel[...] = mask_bf16(jnp.logical_and(b - PAD * q < PIECE, a == b - (PAD - PIECE) * q))

    @pl.when(off_diag)
    def _():
        swap.wait()

    over_z = [send(stage.at[z], stage.at[z], ring_z[d]) for d in (4, 3, 5, 2, 6, 1, 7)]
    a, b = iotas((TOK, TOK))
    hid[...] = nt(mask_bf16(a == b), hidt[...]).astype(BF)
    b, a = iotas((NZ * PAD, FEAT))
    q = (b * 683) >> 16
    selt[...] = mask_bf16(jnp.logical_and(b - PAD * q < PIECE, a == b - (PAD - PIECE) * q))
    for cp in over_z:
        cp.wait_recv()
    et[0] = nn(sel[...], stage[...].reshape(NZ * PAD, TILE)).astype(BF)

    rows2 = [pl.ds(0, HROW), pl.ds(HROW, HROW)]

    def pass_on(src, dst, to, half):
        return send(et.at[src, rows2[half]], et.at[dst, rows2[half]], to)

    a1, a2, a3, b2, b3, c2, c3 = [], [], [], [], [], [], []
    for half in range(2):
        a1.append(pass_on(0, 1, yl, half))
        a2.append(pass_on(0, 6, xp, half))
        a3.append(pass_on(0, 2, xm, half))
    for half in range(2):
        a1[half].wait_recv()
        b2.append(pass_on(1, 7, xp, half))
        b3.append(pass_on(1, 3, xm, half))
        a3[half].wait_recv()
        c3.append(pass_on(2, 4, xm, half))

    def weights(r):
        return jnp.concatenate([et[2 * r], et[2 * r + 1]], axis=1)

    sib_cp, q_cp = {}, {}

    def logits(r):
        s = nn(hid[...], weights(r))
        base = lax.rem(x + r, NX) * 2
        _, lane = iotas((TILE, WIDE))
        block = base + jnp.where(lane < TILE, l, 1 - l)
        for t in range(NH):
            off = jnp.logical_and(block == v, pat[0:1, t : t + 1] == 0)
            part = jnp.where(off, DEAD, s[t * TILE : (t + 1) * TILE])
            sbuf[r, t] = part.reshape(NC, HALF, WIDE)
        sib_cp[r] = send(sbuf.at[r, :, 1 - c], sib.at[r], sibling)

    def mine(r, dq):
        t = add(h, dq, NH)
        return sbuf[r, t, c] + sib[r, t]

    def spread(r):
        sib_cp[r].wait_recv()
        q_cp[r] = []
        for dq in (2, 1, 3):
            s = mine(r, dq)
            dead = s < 0.5 * DEAD
            peak = largest(jnp.where(dead, 0.0, jnp.abs(s)))
            step = jnp.maximum(peak, 1e-30) * (1.0 / TOP)
            steps = jnp.clip(jnp.round(s * (1.0 / step)), -TOP, TOP)
            qout[r, dq - 1] = jnp.where(dead, -TOP - 1.0, steps).astype(jnp.int32).astype(I16)
            qstep[r, dq - 1] = jnp.broadcast_to(step, (8, TILE))
            q_cp[r].append(send(qstep.at[r, dq - 1], qin_step.at[r, dq - 1], ring_h[dq]))
            q_cp[r].append(send(qout.at[r, dq - 1], qin.at[r, dq - 1], ring_h[dq]))

    def whole(r):
        total = mine(r, 0)
        for cp in q_cp[r]:
            cp.wait_recv()
        for k in range(NH - 1):
            steps = qin[r, k].astype(jnp.int32).astype(F32)
            total = total + jnp.where(steps < -TOP - 0.5, DEAD, steps * qin_step[r, k, 0:1, 0:1])
        lsum[r] = total

    logits(0)
    b2[0].wait_recv()
    c2.append(pass_on(7, 5, xp, 0))
    spread(0)
    b2[1].wait_recv()
    c2.append(pass_on(7, 5, xp, 1))
    for cp in b3:
        cp.wait_recv()
    logits(1)
    for cp in a2:
        cp.wait_recv()
    logits(3)
    spread(1)
    spread(3)
    for cp in c3 + c2:
        cp.wait_recv()
    logits(2)
    whole(0)
    spread(2)
    whole(1)
    whole(3)
    whole(2)

    sub, lane = iotas((HALF, TILE))
    turn = sub + c * HALF == lane

    def column(row):
        return jnp.sum(jnp.where(turn, row, 0.0), axis=1, keepdims=True)

    target = column(tgt[pl.ds(h, 1), :].astype(F32)).astype(jnp.int32)
    scale = column(lgr[pl.ds(h, 1), :])
    _, lane2 = iotas((HALF, WIDE))
    hits, ls = [], []
    for r in range(NX):
        col = lax.rem(x + r, NX) * WIDE + jnp.where(lane2 < TILE, l, 1 - l) * TILE
        hits.append(col + jnp.where(lane2 < TILE, lane2, lane2 - TILE) == target)
        ls.append(lsum[r])
    peak = jnp.maximum(jnp.maximum(ls[0], ls[1]), jnp.maximum(ls[2], ls[3]))
    peak = jnp.max(peak, axis=1, keepdims=True)
    total = jnp.sum(sum(jnp.exp(s - peak) for s in ls), axis=1, keepdims=True)
    lse = peak + jnp.log(total)
    at_target = sum(jnp.where(hit, s, 0.0) for hit, s in zip(hits, ls))
    loss = lse - jnp.sum(at_target, axis=1, keepdims=True)
    g_cp, relay = {}, {}
    for r in (2, 1, 3, 0):
        probs = jnp.exp(ls[r] - lse)
        gbuf[r, h, c] = (scale * (probs - jnp.where(hits[r], 1.0, 0.0))).astype(BF)
        own = gbuf.at[r, h, c]
        g_cp[r] = [send(own, own, ring_h[dq]) for dq in (2, 1, 3)]
    loss_row = jnp.sum(jnp.where(turn, loss, 0.0), axis=0, keepdims=True)
    lbuf[v] = jnp.broadcast_to(loss_row, (8, TILE))
    loss_cp = [send(lbuf.at[v], lbuf.at[v], who) for who in others_dev]

    def pair(r):
        for cp in g_cp[r]:
            cp.wait_recv()
        part = gbuf.at[r, :, c]
        relay[r] = send(part, part, sibling)

    def grad(r):
        relay[r].wait_recv()
        return nn(hidt[...], gbuf[r].reshape(TOK, WIDE))

    pair(2)
    d = grad(2)
    xo[0] = d[:, :TILE].astype(BF)
    far_p = send(xo.at[0], xin.at[0], xp)
    xo[1] = d[:, TILE:].astype(BF)
    far_m = send(xo.at[1], xin.at[1], xm)
    pair(1)
    d = grad(1)
    xo[2] = d[:, TILE:].astype(BF)
    p1 = send(xo.at[2], xin.at[2], xp)
    tbuf[0] = d[:, :TILE]
    pair(3)
    d = grad(3)
    xo[3] = d[:, :TILE].astype(BF)
    m0 = send(xo.at[3], xin.at[3], xm)
    tbuf[1] = d[:, TILE:]
    pair(0)
    far_p.wait_recv()
    xs[0] = (tbuf[0] + xin[0].astype(F32)).astype(BF)
    p0 = send(xs.at[0], xin.at[4], xp)
    far_m.wait_recv()
    xs[1] = (tbuf[1] + xin[1].astype(F32)).astype(BF)
    m1 = send(xs.at[1], xin.at[5], xm)
    d = grad(0)
    tbuf[0] = d[:, :TILE]
    tbuf[1] = d[:, TILE:]

    hg = nt(weights(0), gbuf[0].reshape(TOK, WIDE))
    for r in range(1, NX):
        hg = hg + nt(weights(r), gbuf[r].reshape(TOK, WIDE))
    hg_o[...] = hg.astype(BF)
    for cp in loss_cp:
        cp.wait_recv()
    for t in range(NH):
        loss_o[t : t + 1, :] = lbuf[2 * t, 0:1, :] + lbuf[2 * t + 1, 0:1, :]

    z_cp = [[], []]
    for m, (near, far) in ((1, (p1, m1)), (0, (m0, p0))):
        near.wait_recv()
        far.wait_recv()
        tot = tbuf[m] + xin[(3, 2)[m]].astype(F32) + xin[(4, 5)[m]].astype(F32)
        pieces[m] = nn(selt[...], tot.astype(BF)).astype(BF).reshape(NZ, PAD, TILE)
        for d in (4, 3, 5, 2, 6, 1, 7):
            z_cp[m].append(send(pieces.at[m, add(z, d, NZ)], pin.at[m, z], ring_z[d]))
        pin[m, z] = pieces[m, z]

    def over_z_sum(m):
        for cp in z_cp[m]:
            cp.wait_recv()
        total = pin[m, 0].astype(F32)
        for k in range(1, NZ):
            total = total + pin[m, k].astype(F32)
        zsum[m] = total.astype(BF)

    over_z_sum(1)
    end1 = send(zsum.at[1], fin.at[1], away)
    over_z_sum(0)
    end0 = copy(zsum.at[0], fin.at[0], turned)

    @pl.when(off_diag)
    def _():
        end0.start()

    @pl.when(diag)
    def _():
        fin[0] = zsum[0]

    end1.wait_recv()

    @pl.when(off_diag)
    def _():
        end0.wait()

    eg_o[...] = (fin[0].astype(F32) + fin[1].astype(F32))[:PIECE]
    for cp in sent:
        cp.wait_send()


def on_device(hidden, embedding, targets, pattern, loss_grad):
    vmem = pl.BlockSpec(memory_space=pltpu.VMEM)
    loss, hidden_grad, embedding_grad = pl.pallas_call(
        kernel,
        out_shape=(
            jax.ShapeDtypeStruct((NH, TILE), F32),
            jax.ShapeDtypeStruct((FEAT, TOK), BF),
            jax.ShapeDtypeStruct((PIECE, TILE), F32),
        ),
        in_specs=[vmem] * 5,
        out_specs=(vmem,) * 3,
        scratch_shapes=[
            pltpu.VMEM((PAD, TILE), BF),
            pltpu.VMEM((NZ, PAD, TILE), BF),
            pltpu.VMEM((FEAT, NZ * PAD), BF),
            pltpu.VMEM((NZ * PAD, FEAT), BF),
            pltpu.VMEM((TOK, FEAT), BF),
            pltpu.VMEM((8, FEAT, TILE), BF),
            pltpu.VMEM((NX, NH, NC, HALF, WIDE), F32),
            pltpu.VMEM((NX, NH, HALF, WIDE), F32),
            pltpu.VMEM((NX, NH - 1, HALF, WIDE), I16),
            pltpu.VMEM((NX, NH - 1, 8, TILE), F32),
            pltpu.VMEM((NX, NH - 1, HALF, WIDE), I16),
            pltpu.VMEM((NX, NH - 1, 8, TILE), F32),
            pltpu.VMEM((NX, HALF, WIDE), F32),
            pltpu.VMEM((NX, NH, NC, HALF, WIDE), BF),
            pltpu.VMEM((NH * NC, 8, TILE), F32),
            pltpu.VMEM((4, FEAT, TILE), BF),
            pltpu.VMEM((2, FEAT, TILE), BF),
            pltpu.VMEM((6, FEAT, TILE), BF),
            pltpu.VMEM((2, FEAT, TILE), F32),
            pltpu.VMEM((2, NZ, PAD, TILE), BF),
            pltpu.VMEM((2, NZ, PAD, TILE), BF),
            pltpu.VMEM((2, PAD, TILE), BF),
            pltpu.VMEM((2, PAD, TILE), BF),
            pltpu.SemaphoreType.DMA((NSEM,)),
            pltpu.SemaphoreType.DMA((NSEM,)),
        ],
        compiler_params=pltpu.CompilerParams(
            collective_id=0, has_side_effects=True, vmem_limit_bytes=48 << 20
        ),
    )(hidden.T, embedding.T, targets.reshape(NH, TILE), pattern.T, loss_grad.reshape(NH, TILE))
    return loss.reshape(TOK), hidden_grad.T, embedding_grad.T


def solution(mesh):
    return jax.shard_map(
        on_device,
        mesh=mesh,
        in_specs=(
            P(("dp", "ctx"), "vocab"),
            P("vocab", ("dp", "ctx")),
            P(("dp", "ctx")),
            P(("dp", "ctx"), "vocab"),
            P(("dp", "ctx")),
        ),
        out_specs=(P(("dp", "ctx")), P(("dp", "ctx"), "vocab"), P("vocab", ("dp", "ctx"))),
        check_vma=False,
    )
```

```python
import jax
import jax.numpy as jnp
from jax import lax
from jax.experimental import pallas as pl
from jax.experimental.pallas import tpu as pltpu
from jax.sharding import PartitionSpec as P

MESH = pl.DeviceIdType.MESH
BF = jnp.bfloat16
F32 = jnp.float32
I16 = jnp.int16
DEAD = -1e30
TOP = 32767.0
NX, NL, NZ, NH, NC = 4, 2, 8, 4, 2
TILE = 128
HALF = 64
WIDE = 2 * TILE
TOK = 512
FEAT = 672
PIECE = 84
PAD = 96
NSEM = 192
ORDER_Z = (1, 7, 2, 6, 3, 5, 4)


def nt(a, b):
    return lax.dot_general(a, b, (((1,), (1,)), ((), ())), preferred_element_type=F32)


def tn(a, b):
    return lax.dot_general(a, b, (((0,), (0,)), ((), ())), preferred_element_type=F32)


def nn(a, b):
    return jnp.dot(a, b, preferred_element_type=F32)


def iotas(shape):
    return lax.broadcasted_iota(jnp.int32, shape, 0), lax.broadcasted_iota(jnp.int32, shape, 1)


def largest(a):
    return jnp.max(jnp.max(a, axis=1, keepdims=True), axis=0, keepdims=True)


def kernel(
    hidt_in, embt_in, tgt_in, pat_in, lgr_in, loss_o, hg_o, eg_o,
    hidt, embt, tgt, pat, lgr, hidp, piece, et, sbuf, sib, qout, qstep, qin, qin_step, lsum,
    gbuf, lbuf, xo, xin, pieces, pin, zsum, fin, ssem, rsem, lsem,
):
    x = lax.axis_index("dp")
    ctx = lax.axis_index("ctx")
    v = lax.axis_index("vocab")
    l, z = lax.div(ctx, NZ), lax.rem(ctx, NZ)
    h, c = lax.div(v, NC), lax.rem(v, NC)

    def dev(x, l, z, h, c):
        return (x, l * NZ + z, h * NC + c)

    def add(a, d, n):
        return lax.rem(a + d, n)

    sibling = dev(x, l, z, h, 1 - c)
    ring_h = [dev(x, l, z, add(h, dq, NH), c) for dq in range(NH)]
    xp, xm = dev(add(x, 1, NX), l, z, h, c), dev(add(x, 3, NX), l, z, h, c)
    yl = dev(x, 1 - l, z, h, c)
    ring_z = [dev(x, l, add(z, d, NZ), h, c) for d in range(NZ)]
    turned = dev(h, c, z, x, l)
    away, away_src = dev(h, c, z, x, 1 - l), dev(h, 1 - c, z, x, l)
    x2, h2 = add(x, 2, NX), add(h, 2, NX)
    far = [dev(x2, l, z, h, c), dev(x2, 1 - l, z, h, c)]
    far_away = [dev(h, c, z, x2, l), dev(h, c, z, x2, 1 - l)]
    far_away_src = [dev(h2, c, z, x, l), dev(h2, 1 - c, z, x, l)]
    diag = jnp.logical_and(x == h, l == c)
    off_diag = jnp.logical_not(diag)

    bar = pltpu.get_barrier_semaphore()

    def greet(who):
        pl.semaphore_signal(bar, inc=1, device_id=who, device_id_type=MESH)

    others = [(dq, dc) for dq in range(NH) for dc in range(NC) if dq or dc]
    others_dev = [dev(x, l, z, add(h, dq, NH), add(c, dc, NC)) for dq, dc in others]
    met = others_dev + [xp, xm, yl] + ring_z[1:] + far + far_away_src + [away_src]

    @pl.when(off_diag)
    def _():
        greet(turned)

    for who in met:
        greet(who)

    count = [0]
    sent = []

    def copy(src, dst, to):
        i = count[0]
        count[0] += 1
        cp = pltpu.make_async_remote_copy(
            src_ref=src, dst_ref=dst, send_sem=ssem.at[i], recv_sem=rsem.at[i],
            device_id=to, device_id_type=MESH,
        )
        return cp

    def send(src, dst, to):
        cp = copy(src, dst, to)
        cp.start()
        sent.append(cp)
        return cp

    loads = [
        pltpu.make_async_copy(src, dst, lsem.at[i])
        for i, (src, dst) in enumerate(
            ((embt_in, embt), (hidt_in, hidt), (tgt_in, tgt), (pat_in, pat), (lgr_in, lgr))
        )
    ]
    for cp in loads:
        cp.start()
    piece[...] = jnp.zeros((PAD, TILE), BF)
    loads[0].wait()
    piece[:PIECE] = embt[...]
    pl.semaphore_wait(bar, jnp.where(off_diag, len(met) + 1, len(met)))
    swap = copy(piece, et.at[0, z], turned)

    @pl.when(off_diag)
    def _():
        swap.start()

    @pl.when(diag)
    def _():
        et[0, z] = piece[...]

    for cp in loads[1:]:
        cp.wait()
    hidp[...] = jnp.zeros((NZ, PAD, TOK), BF)
    for k in range(NZ):
        hidp[k, :PIECE] = hidt[k * PIECE : (k + 1) * PIECE]

    @pl.when(off_diag)
    def _():
        swap.wait()


    def over_z(slot):
        own = et.at[slot, z]
        return {d: send(own, own, ring_z[d]) for d in ORDER_Z}

    z_own = over_z(0)
    a1, a2, a3, b2, b3 = {}, {}, {}, {}, {}

    def pass_on(src, dst, to, d):
        k = add(z, d, NZ)
        return send(et.at[src, k], et.at[dst, k], to)

    def spread_own(d):
        if d:
            z_own[NZ - d].wait_recv()
        a1[d] = pass_on(0, 1, yl, d)
        a2[d] = pass_on(0, 6, xp, d)
        a3[d] = pass_on(0, 2, xm, d)

    def spread_yl(d):
        a1[d].wait_recv()
        b2[d] = pass_on(1, 7, xp, d)
        b3[d] = pass_on(1, 3, xm, d)

    spread_own(0)
    far_in = [send(et.at[0, z], et.at[4 + m, z], far[m]) for m in range(2)]
    spread_own(1)
    spread_own(7)
    spread_yl(0)
    z_far = []
    for m in range(2):
        far_in[m].wait_recv()
        z_far.append(over_z(4 + m))
    spread_own(2)
    spread_own(6)
    spread_yl(1)
    spread_yl(7)
    spread_own(3)
    spread_own(5)
    spread_yl(2)
    spread_yl(6)
    spread_own(4)
    spread_yl(3)
    spread_yl(5)
    spread_yl(4)

    def weights(r):
        parts = [et[2 * r + m].reshape(NZ * PAD, TILE) for m in range(2)]
        return jnp.concatenate(parts, axis=1)

    sib_cp, q_cp = {}, {}

    def logits(r):
        s = tn(hidp[...].reshape(NZ * PAD, TOK), weights(r))
        base = lax.rem(x + r, NX) * 2
        _, lane = iotas((TILE, WIDE))
        block = base + jnp.where(lane < TILE, l, 1 - l)
        for t in range(NH):
            off = jnp.logical_and(block == v, pat[0:1, t : t + 1] == 0)
            part = jnp.where(off, DEAD, s[t * TILE : (t + 1) * TILE])
            sbuf[r, t] = part.reshape(NC, HALF, WIDE)
        sib_cp[r] = send(sbuf.at[r, :, 1 - c], sib.at[r], sibling)

    def mine(r, dq):
        t = add(h, dq, NH)
        return sbuf[r, t, c] + sib[r, t]

    def spread(r):
        sib_cp[r].wait_recv()
        q_cp[r] = []
        for dq in (2, 1, 3):
            s = mine(r, dq)
            dead = s < 0.5 * DEAD
            peak = largest(jnp.where(dead, 0.0, jnp.abs(s)))
            step = jnp.maximum(peak, 1e-30) * (1.0 / TOP)
            steps = jnp.clip(jnp.round(s * (1.0 / step)), -TOP, TOP)
            qout[r, dq - 1] = jnp.where(dead, -TOP - 1.0, steps).astype(jnp.int32).astype(I16)
            qstep[r, dq - 1] = jnp.broadcast_to(step, (8, TILE))
            q_cp[r].append(send(qstep.at[r, dq - 1], qin_step.at[r, dq - 1], ring_h[dq]))
            q_cp[r].append(send(qout.at[r, dq - 1], qin.at[r, dq - 1], ring_h[dq]))

    def whole(r):
        total = mine(r, 0)
        for cp in q_cp[r]:
            cp.wait_recv()
        for k in range(NH - 1):
            steps = qin[r, k].astype(jnp.int32).astype(F32)
            total = total + jnp.where(steps < -TOP - 0.5, DEAD, steps * qin_step[r, k, 0:1, 0:1])
        lsum[r] = total

    logits(0)
    spread(0)
    for d in range(NZ):
        a3[d].wait_recv()
        b3[d].wait_recv()
    logits(1)
    for d in range(NZ):
        a2[d].wait_recv()
        b2[d].wait_recv()
    logits(3)
    spread(1)
    spread(3)
    for m in range(2):
        for d in ORDER_Z:
            z_far[m][d].wait_recv()
    logits(2)
    whole(0)
    spread(2)
    whole(1)
    whole(3)
    whole(2)

    sub, lane = iotas((HALF, TILE))
    turn = sub + c * HALF == lane

    def column(row):
        return jnp.sum(jnp.where(turn, row, 0.0), axis=1, keepdims=True)

    target = column(tgt[pl.ds(h, 1), :].astype(F32)).astype(jnp.int32)
    scale = column(lgr[pl.ds(h, 1), :])
    _, lane2 = iotas((HALF, WIDE))
    hits, ls = [], []
    for r in range(NX):
        col = lax.rem(x + r, NX) * WIDE + jnp.where(lane2 < TILE, l, 1 - l) * TILE
        hits.append(col + jnp.where(lane2 < TILE, lane2, lane2 - TILE) == target)
        ls.append(lsum[r])
    peak = jnp.maximum(jnp.maximum(ls[0], ls[1]), jnp.maximum(ls[2], ls[3]))
    peak = jnp.max(peak, axis=1, keepdims=True)
    total = jnp.sum(sum(jnp.exp(s - peak) for s in ls), axis=1, keepdims=True)
    lse = peak + jnp.log(total)
    at_target = sum(jnp.where(hit, s, 0.0) for hit, s in zip(hits, ls))
    loss = lse - jnp.sum(at_target, axis=1, keepdims=True)
    g_cp, relay = {}, {}
    for r in (1, 3, 2, 0):
        probs = jnp.exp(ls[r] - lse)
        gbuf[r, h, c] = (scale * (probs - jnp.where(hits[r], 1.0, 0.0))).astype(BF)
        own = gbuf.at[r, h, c]
        g_cp[r] = [send(own, own, ring_h[dq]) for dq in (2, 1, 3)]
    loss_row = jnp.sum(jnp.where(turn, loss, 0.0), axis=0, keepdims=True)
    lbuf[v] = jnp.broadcast_to(loss_row, (8, TILE))
    loss_cp = [send(lbuf.at[v], lbuf.at[v], who) for who in others_dev]

    def pair(r):
        for cp in g_cp[r]:
            cp.wait_recv()
        part = gbuf.at[r, :, c]
        relay[r] = send(part, part, sibling)

    def grad(r):
        relay[r].wait_recv()
        return nn(hidt[...], gbuf[r].reshape(TOK, WIDE))

    def to_near(r, to):
        d = grad(r)
        out = []
        for m in range(2):
            xo[r // 2, m] = d[:, m * TILE : (m + 1) * TILE].astype(BF)
            out.append(send(xo.at[r // 2, m], xin.at[r // 2, m], to))
        return out

    def to_z(slot, tot):
        for k in range(NZ):
            pieces[slot, k, :PIECE] = tot[k * PIECE : (k + 1) * PIECE].astype(BF)
        pin[slot, z] = pieces[slot, z]
        return [send(pieces.at[slot, add(z, d, NZ)], pin.at[slot, z], ring_z[d]) for d in ORDER_Z]

    def sum_z(slot, cps):
        for cp in cps:
            cp.wait_recv()
        total = pin[slot, 0].astype(F32)
        for k in range(1, NZ):
            total = total + pin[slot, k].astype(F32)
        zsum[slot] = total.astype(BF)

    pieces[...] = jnp.zeros((4, NZ, PAD, TILE), BF)
    pair(1)
    near_p = to_near(1, xp)
    pair(3)
    near_m = to_near(3, xm)
    pair(2)
    d = grad(2)
    z_cp = {2 + m: to_z(2 + m, d[:, m * TILE : (m + 1) * TILE]) for m in range(2)}
    pair(0)
    own = grad(0)
    for m in range(2):
        near_p[m].wait_recv()
        near_m[m].wait_recv()
        near = xin[0, m].astype(F32) + xin[1, m].astype(F32)
        z_cp[m] = to_z(m, own[:, m * TILE : (m + 1) * TILE] + near)

    hg = nt(weights(0), gbuf[0].reshape(TOK, WIDE))
    for r in range(1, NX):
        hg = hg + nt(weights(r), gbuf[r].reshape(TOK, WIDE))
    for k in range(NZ):
        hg_o[k * PIECE : (k + 1) * PIECE] = hg[k * PAD : k * PAD + PIECE].astype(BF)
    for cp in loss_cp:
        cp.wait_recv()
    for t in range(NH):
        loss_o[t : t + 1, :] = lbuf[2 * t, 0:1, :] + lbuf[2 * t + 1, 0:1, :]

    end = {}
    for slot in (2, 3):
        sum_z(slot, z_cp[slot])
        end[slot] = send(zsum.at[slot], fin.at[slot], far_away[slot - 2])
    sum_z(0, z_cp[0])
    end0 = copy(zsum.at[0], fin.at[0], turned)

    @pl.when(off_diag)
    def _():
        end0.start()

    @pl.when(diag)
    def _():
        fin[0] = zsum[0]

    sum_z(1, z_cp[1])
    end[1] = send(zsum.at[1], fin.at[1], away)
    for cp in end.values():
        cp.wait_recv()

    @pl.when(off_diag)
    def _():
        end0.wait()

    total = fin[0].astype(F32)
    for slot in range(1, 4):
        total = total + fin[slot].astype(F32)
    eg_o[...] = total[:PIECE]
    for cp in sent:
        cp.wait_send()


def on_device(hidden, embedding, targets, pattern, loss_grad):
    vmem = pl.BlockSpec(memory_space=pltpu.VMEM)
    loss, hidden_grad, embedding_grad = pl.pallas_call(
        kernel,
        out_shape=(
            jax.ShapeDtypeStruct((NH, TILE), F32),
            jax.ShapeDtypeStruct((FEAT, TOK), BF),
            jax.ShapeDtypeStruct((PIECE, TILE), F32),
        ),
        in_specs=[pl.BlockSpec(memory_space=pltpu.HBM)] * 5,
        out_specs=(vmem,) * 3,
        scratch_shapes=[
            pltpu.VMEM((FEAT, TOK), BF),
            pltpu.VMEM((PIECE, TILE), BF),
            pltpu.VMEM((NH, TILE), jnp.int32),
            pltpu.VMEM((1, NH), jnp.int32),
            pltpu.VMEM((NH, TILE), F32),
            pltpu.VMEM((NZ, PAD, TOK), BF),
            pltpu.VMEM((PAD, TILE), BF),
            pltpu.VMEM((8, NZ, PAD, TILE), BF),
            pltpu.VMEM((NX, NH, NC, HALF, WIDE), F32),
            pltpu.VMEM((NX, NH, HALF, WIDE), F32),
            pltpu.VMEM((NX, NH - 1, HALF, WIDE), I16),
            pltpu.VMEM((NX, NH - 1, 8, TILE), F32),
            pltpu.VMEM((NX, NH - 1, HALF, WIDE), I16),
            pltpu.VMEM((NX, NH - 1, 8, TILE), F32),
            pltpu.VMEM((NX, HALF, WIDE), F32),
            pltpu.VMEM((NX, NH, NC, HALF, WIDE), BF),
            pltpu.VMEM((NH * NC, 8, TILE), F32),
            pltpu.VMEM((2, 2, FEAT, TILE), BF),
            pltpu.VMEM((2, 2, FEAT, TILE), BF),
            pltpu.VMEM((4, NZ, PAD, TILE), BF),
            pltpu.VMEM((4, NZ, PAD, TILE), BF),
            pltpu.VMEM((4, PAD, TILE), BF),
            pltpu.VMEM((4, PAD, TILE), BF),
            pltpu.SemaphoreType.DMA((NSEM,)),
            pltpu.SemaphoreType.DMA((NSEM,)),
            pltpu.SemaphoreType.DMA((5,)),
        ],
        compiler_params=pltpu.CompilerParams(
            collective_id=0, has_side_effects=True, vmem_limit_bytes=48 << 20
        ),
    )(hidden.T, embedding.T, targets.reshape(NH, TILE), pattern.T, loss_grad.reshape(NH, TILE))
    return loss.reshape(TOK), hidden_grad.T, embedding_grad.T


def solution(mesh):
    return jax.shard_map(
        on_device,
        mesh=mesh,
        in_specs=(
            P(("dp", "ctx"), "vocab"),
            P("vocab", ("dp", "ctx")),
            P(("dp", "ctx")),
            P(("dp", "ctx"), "vocab"),
            P(("dp", "ctx")),
        ),
        out_specs=(P(("dp", "ctx")), P(("dp", "ctx"), "vocab"), P("vocab", ("dp", "ctx"))),
        check_vma=False,
    )
```

```python
import jax
import jax.numpy as jnp
from jax import lax
from jax.experimental import pallas as pl
from jax.experimental.pallas import tpu as pltpu
from jax.sharding import PartitionSpec as P

MESH = pl.DeviceIdType.MESH
BF = jnp.bfloat16
F32 = jnp.float32
I16 = jnp.int16
DEAD = -1e30
TOP = 32767.0
NX, NL, NZ, NH, NC = 4, 2, 8, 4, 2
TILE = 128
HALF = 64
WIDE = 2 * TILE
TOK = 512
FEAT = 672
PIECE = 84
PAD = 96
NSEM = 64
BLOCKS = ((0, 0), (0, 1), (1, 0), (3, 0), (1, 1), (3, 1), (2, 0), (2, 1))
ORDER_Z = (1, 7, 2, 6, 3, 5, 4)


def nt(a, b):
    return lax.dot_general(a, b, (((1,), (1,)), ((), ())), preferred_element_type=F32)


def tn(a, b):
    return lax.dot_general(a, b, (((0,), (0,)), ((), ())), preferred_element_type=F32)


def nn(a, b):
    return jnp.dot(a, b, preferred_element_type=F32)


def iotas(shape):
    return lax.broadcasted_iota(jnp.int32, shape, 0), lax.broadcasted_iota(jnp.int32, shape, 1)


def largest(a):
    return jnp.max(jnp.max(a, axis=1, keepdims=True), axis=0, keepdims=True)


def kernel(
    hidt, embt, tgt, pat, lgr, loss_o, hg_o, eg_o,
    hidp, piece, et, sbuf, sib, qout, qstep, qin, qin_step, lsum,
    gbuf, lbuf, xo, xin, pieces, pin, zsum, fin, ssem, rsem,
):
    x = lax.axis_index("dp")
    ctx = lax.axis_index("ctx")
    v = lax.axis_index("vocab")
    l, z = lax.div(ctx, NZ), lax.rem(ctx, NZ)
    h, c = lax.div(v, NC), lax.rem(v, NC)

    def dev(x, l, z, h, c):
        return (x, l * NZ + z, h * NC + c)

    def add(a, d, n):
        return lax.rem(a + d, n)

    sibling = dev(x, l, z, h, 1 - c)
    ring_h = [dev(x, l, z, add(h, dq, NH), c) for dq in range(NH)]
    xp, xm = dev(add(x, 1, NX), l, z, h, c), dev(add(x, 3, NX), l, z, h, c)
    yl = dev(x, 1 - l, z, h, c)
    ring_z = [dev(x, l, add(z, d, NZ), h, c) for d in range(NZ)]
    turned = dev(h, c, z, x, l)
    away, away_src = dev(h, c, z, x, 1 - l), dev(h, 1 - c, z, x, l)
    x2, h2 = add(x, 2, NX), add(h, 2, NX)
    far = [dev(x2, l, z, h, c), dev(x2, 1 - l, z, h, c)]
    far_away = [dev(h, c, z, x2, l), dev(h, c, z, x2, 1 - l)]
    far_away_src = [dev(h2, c, z, x, l), dev(h2, 1 - c, z, x, l)]
    diag = jnp.logical_and(x == h, l == c)
    off_diag = jnp.logical_not(diag)

    bar = pltpu.get_barrier_semaphore()

    def greet(who):
        pl.semaphore_signal(bar, inc=1, device_id=who, device_id_type=MESH)

    others = [(dq, dc) for dq in range(NH) for dc in range(NC) if dq or dc]
    others_dev = [dev(x, l, z, add(h, dq, NH), add(c, dc, NC)) for dq, dc in others]
    met = others_dev + [xp, xm, yl] + ring_z[1:] + far + far_away_src + [away_src]

    @pl.when(off_diag)
    def _():
        greet(turned)

    for who in met:
        greet(who)

    count = [0]
    sent = []

    def group():
        count[0] += 1
        return count[0] - 1

    def copy(src, dst, to, i):
        return pltpu.make_async_remote_copy(
            src_ref=src, dst_ref=dst, send_sem=ssem.at[i], recv_sem=rsem.at[i],
            device_id=to, device_id_type=MESH,
        )

    def wait_in(ref, i):
        copy(ref, ref, sibling, i).wait_recv()

    def wait_out(ref, i):
        copy(ref, ref, sibling, i).wait_send()

    def send_all(copies, ref):
        i = group()
        for src, dst, to in copies:
            copy(src, dst, to, i).start()
        sent.append((ref, i))
        return ref, i

    def send(src, dst, to):
        return send_all([(src, dst, to)], src)

    piece[...] = jnp.zeros((PAD, TILE), BF)
    piece[:PIECE] = embt[...]
    pl.semaphore_wait(bar, jnp.where(off_diag, len(met) + 1, len(met)))
    swap = copy(piece, et.at[0, z], turned, group())

    @pl.when(off_diag)
    def _():
        swap.start()

    @pl.when(diag)
    def _():
        et[0, z] = piece[...]

    hidp[...] = jnp.zeros((NZ, PAD, TOK), BF)
    for k in range(NZ):
        hidp[k, :PIECE] = hidt[k * PIECE : (k + 1) * PIECE]

    @pl.when(off_diag)
    def _():
        swap.wait()


    def index(d):
        return add(z, d, NZ)

    z_own = {d: send(et.at[0, z], et.at[0, z], ring_z[d]) for d in ORDER_Z}
    a1, groups = {}, [group() for _ in range(4)]

    def pass_on(src, dst, to, d, i):
        copy(et.at[src, index(d)], et.at[dst, index(d)], to, i).start()

    def spread_own(d):
        if d:
            wait_in(*z_own[NZ - d])
        part = et.at[0, index(d)]
        a1[d] = send(part, et.at[1, index(d)], yl)
        pass_on(0, 3, xp, d, groups[0])
        pass_on(0, 2, xm, d, groups[1])

    def spread_yl(d):
        wait_in(*a1[d])
        pass_on(1, 5, xp, d, groups[2])
        pass_on(1, 4, xm, d, groups[3])

    spread_own(0)
    far_in = [send(et.at[0, z], et.at[6 + m, z], far[m]) for m in range(2)]
    spread_own(1)
    spread_own(7)
    spread_yl(0)
    z_far = []
    for m in range(2):
        wait_in(*far_in[m])
        part = et.at[6 + m, z]
        copies = [(part, part, ring_z[d]) for d in ORDER_Z]
        z_far.append(send_all(copies, et.at[6 + m, pl.ds(0, NZ - 1)]))
    spread_own(2)
    spread_own(6)
    spread_yl(1)
    spread_yl(7)
    spread_own(3)
    spread_own(5)
    spread_yl(2)
    spread_yl(6)
    spread_own(4)
    spread_yl(3)
    spread_yl(5)
    spread_yl(4)
    for k, slot in enumerate((3, 2, 5, 4)):
        sent.append((et.at[slot], groups[k]))

    def weights(r):
        parts = [et[2 * r + m].reshape(NZ * PAD, TILE) for m in range(2)]
        return jnp.concatenate(parts, axis=1)

    def block_of(slot):
        dx, m = BLOCKS[slot]
        return 2 * add(x, dx, NX) + (1 - l if m else l)

    sib_cp, q_cp = {}, {}

    def logits(r):
        s = tn(hidp[...].reshape(NZ * PAD, TOK), weights(r))
        _, lane = iotas((TILE, WIDE))
        block = jnp.where(lane < TILE, block_of(2 * r), block_of(2 * r + 1))
        for t in range(NH):
            off = jnp.logical_and(block == v, pat[0:1, t : t + 1] == 0)
            part = jnp.where(off, DEAD, s[t * TILE : (t + 1) * TILE])
            sbuf[r, t] = part.reshape(NC, HALF, WIDE)
        sib_cp[r] = send(sbuf.at[r, :, 1 - c], sib.at[r], sibling)

    def mine(r, dq):
        t = add(h, dq, NH)
        return sbuf[r, t, c] + sib[r, t]

    def spread(r):
        wait_in(*sib_cp[r])
        tiles, steps = [], []
        for dq in (2, 1, 3):
            s = mine(r, dq)
            dead = s < 0.5 * DEAD
            peak = largest(jnp.where(dead, 0.0, jnp.abs(s)))
            step = jnp.maximum(peak, 1e-30) * (1.0 / TOP)
            near = jnp.clip(jnp.round(s * (1.0 / step)), -TOP, TOP)
            qout[r, dq - 1] = jnp.where(dead, -TOP - 1.0, near).astype(jnp.int32).astype(I16)
            qstep[r, dq - 1] = jnp.broadcast_to(step, (8, TILE))
            tiles.append((qout.at[r, dq - 1], qin.at[r, dq - 1], ring_h[dq]))
            steps.append((qstep.at[r, dq - 1], qin_step.at[r, dq - 1], ring_h[dq]))
        q_cp[r] = (send_all(steps, qstep.at[r]), send_all(tiles, qout.at[r]))

    def whole(r):
        total = mine(r, 0)
        for cp in q_cp[r]:
            wait_in(*cp)
        for k in range(NH - 1):
            steps = qin[r, k].astype(jnp.int32).astype(F32)
            total = total + jnp.where(steps < -TOP - 0.5, DEAD, steps * qin_step[r, k, 0:1, 0:1])
        lsum[r] = total

    logits(0)
    spread(0)
    wait_in(et.at[2], groups[1])
    wait_in(et.at[3], groups[0])
    logits(1)
    wait_in(et.at[4], groups[3])
    wait_in(et.at[5], groups[2])
    logits(2)
    spread(1)
    spread(2)
    for m in range(2):
        wait_in(*z_far[m])
    logits(3)
    whole(0)
    spread(3)
    whole(1)
    whole(2)
    whole(3)

    sub, lane = iotas((HALF, TILE))
    turn = sub + c * HALF == lane

    def column(row):
        return jnp.sum(jnp.where(turn, row, 0.0), axis=1, keepdims=True)

    target = column(tgt[pl.ds(h, 1), :].astype(F32)).astype(jnp.int32)
    scale = column(lgr[pl.ds(h, 1), :])
    _, lane2 = iotas((HALF, WIDE))
    hits, ls = [], []
    for r in range(NX):
        col = jnp.where(lane2 < TILE, block_of(2 * r), block_of(2 * r + 1) - 1) * TILE + lane2
        hits.append(col == target)
        ls.append(lsum[r])
    peak = jnp.maximum(jnp.maximum(ls[0], ls[1]), jnp.maximum(ls[2], ls[3]))
    peak = jnp.max(peak, axis=1, keepdims=True)
    total = jnp.sum(sum(jnp.exp(s - peak) for s in ls), axis=1, keepdims=True)
    lse = peak + jnp.log(total)
    at_target = sum(jnp.where(hit, s, 0.0) for hit, s in zip(hits, ls))
    loss = lse - jnp.sum(at_target, axis=1, keepdims=True)
    g_cp, relay = {}, {}
    for r in (3, 1, 2, 0):
        probs = jnp.exp(ls[r] - lse)
        gbuf[r, h, c] = (scale * (probs - jnp.where(hits[r], 1.0, 0.0))).astype(BF)
        own = gbuf.at[r, h, c]
        copies = [(own, own, ring_h[dq]) for dq in (2, 1, 3)]
        g_cp[r] = send_all(copies, gbuf.at[r, pl.ds(0, NH - 1), 0])
    loss_row = jnp.sum(jnp.where(turn, loss, 0.0), axis=0, keepdims=True)
    lbuf[v] = jnp.broadcast_to(loss_row, (8, TILE))
    copies = [(lbuf.at[v], lbuf.at[v], who) for who in others_dev]
    loss_cp = send_all(copies, lbuf.at[pl.ds(0, NH * NC - 1)])

    def pair(r):
        wait_in(*g_cp[r])
        part = gbuf.at[r, :, c]
        relay[r] = send(part, part, sibling)

    def grad(r):
        wait_in(*relay[r])
        return nn(hidt[...], gbuf[r].reshape(TOK, WIDE))

    def to_near(m):
        d = grad(1 + m)
        out = []
        for side, to in enumerate((xp, xm)):
            xo[side, m] = d[:, side * TILE : (side + 1) * TILE].astype(BF)
            out.append(send(xo.at[side, m], xin.at[side, m], to))
        return out

    def to_z(slot, tot):
        for k in range(NZ):
            pieces[slot, k, :PIECE] = tot[k * PIECE : (k + 1) * PIECE].astype(BF)
        pin[slot, z] = pieces[slot, z]
        copies = [(pieces.at[slot, index(d)], pin.at[slot, z], ring_z[d]) for d in ORDER_Z]
        return send_all(copies, pieces.at[slot, pl.ds(0, NZ - 1)])

    def sum_z(slot):
        wait_in(*z_cp[slot])
        total = pin[slot, 0].astype(F32)
        for k in range(1, NZ):
            total = total + pin[slot, k].astype(F32)
        zsum[slot] = total.astype(BF)

    pieces[...] = jnp.zeros((4, NZ, PAD, TILE), BF)
    pair(3)
    d = grad(3)
    z_cp = {2 + m: to_z(2 + m, d[:, m * TILE : (m + 1) * TILE]) for m in range(2)}
    pair(1)
    near = [to_near(0)]
    pair(2)
    near.append(to_near(1))
    pair(0)
    own = grad(0)
    for m in range(2):
        for cp in near[m]:
            wait_in(*cp)
        both = xin[0, m].astype(F32) + xin[1, m].astype(F32)
        z_cp[m] = to_z(m, own[:, m * TILE : (m + 1) * TILE] + both)

    hg = nt(weights(0), gbuf[0].reshape(TOK, WIDE))
    for r in range(1, NX):
        hg = hg + nt(weights(r), gbuf[r].reshape(TOK, WIDE))
    for k in range(NZ):
        hg_o[k * PIECE : (k + 1) * PIECE] = hg[k * PAD : k * PAD + PIECE].astype(BF)
    wait_in(*loss_cp)
    for t in range(NH):
        loss_o[t : t + 1, :] = lbuf[2 * t, 0:1, :] + lbuf[2 * t + 1, 0:1, :]

    end = []
    for slot in (2, 3):
        sum_z(slot)
        end.append(send(zsum.at[slot], fin.at[slot], far_away[slot - 2]))
    sum_z(0)
    end0 = copy(zsum.at[0], fin.at[0], turned, group())

    @pl.when(off_diag)
    def _():
        end0.start()

    @pl.when(diag)
    def _():
        fin[0] = zsum[0]

    sum_z(1)
    end.append(send(zsum.at[1], fin.at[1], away))
    for cp in end:
        wait_in(*cp)

    @pl.when(off_diag)
    def _():
        end0.wait()

    total = fin[0].astype(F32)
    for slot in range(1, 4):
        total = total + fin[slot].astype(F32)
    eg_o[...] = total[:PIECE]
    for cp in sent:
        wait_out(*cp)


def on_device(hidden, embedding, targets, pattern, loss_grad):
    vmem = pl.BlockSpec(memory_space=pltpu.VMEM)
    loss, hidden_grad, embedding_grad = pl.pallas_call(
        kernel,
        out_shape=(
            jax.ShapeDtypeStruct((NH, TILE), F32),
            jax.ShapeDtypeStruct((FEAT, TOK), BF),
            jax.ShapeDtypeStruct((PIECE, TILE), F32),
        ),
        in_specs=[vmem] * 5,
        out_specs=(vmem,) * 3,
        scratch_shapes=[
            pltpu.VMEM((NZ, PAD, TOK), BF),
            pltpu.VMEM((PAD, TILE), BF),
            pltpu.VMEM((8, NZ, PAD, TILE), BF),
            pltpu.VMEM((NX, NH, NC, HALF, WIDE), F32),
            pltpu.VMEM((NX, NH, HALF, WIDE), F32),
            pltpu.VMEM((NX, NH - 1, HALF, WIDE), I16),
            pltpu.VMEM((NX, NH - 1, 8, TILE), F32),
            pltpu.VMEM((NX, NH - 1, HALF, WIDE), I16),
            pltpu.VMEM((NX, NH - 1, 8, TILE), F32),
            pltpu.VMEM((NX, HALF, WIDE), F32),
            pltpu.VMEM((NX, NH, NC, HALF, WIDE), BF),
            pltpu.VMEM((NH * NC, 8, TILE), F32),
            pltpu.VMEM((2, 2, FEAT, TILE), BF),
            pltpu.VMEM((2, 2, FEAT, TILE), BF),
            pltpu.VMEM((4, NZ, PAD, TILE), BF),
            pltpu.VMEM((4, NZ, PAD, TILE), BF),
            pltpu.VMEM((4, PAD, TILE), BF),
            pltpu.VMEM((4, PAD, TILE), BF),
            pltpu.SemaphoreType.DMA((NSEM,)),
            pltpu.SemaphoreType.DMA((NSEM,)),
        ],
        compiler_params=pltpu.CompilerParams(
            collective_id=0, has_side_effects=True, vmem_limit_bytes=48 << 20
        ),
    )(hidden.T, embedding.T, targets.reshape(NH, TILE), pattern.T, loss_grad.reshape(NH, TILE))
    return loss.reshape(TOK), hidden_grad.T, embedding_grad.T


def solution(mesh):
    return jax.shard_map(
        on_device,
        mesh=mesh,
        in_specs=(
            P(("dp", "ctx"), "vocab"),
            P("vocab", ("dp", "ctx")),
            P(("dp", "ctx")),
            P(("dp", "ctx"), "vocab"),
            P(("dp", "ctx")),
        ),
        out_specs=(P(("dp", "ctx")), P(("dp", "ctx"), "vocab"), P("vocab", ("dp", "ctx"))),
        check_vma=False,
    )
```

```python
import jax
import jax.numpy as jnp
from jax import lax
from jax.experimental import pallas as pl
from jax.experimental.pallas import tpu as pltpu
from jax.sharding import PartitionSpec as P

MESH = pl.DeviceIdType.MESH
BF = jnp.bfloat16
F32 = jnp.float32
I16 = jnp.int16
DEAD = -1e30
TOP = 32767.0
NX, NL, NZ, NH, NC = 4, 2, 8, 4, 2
TILE = 128
HALF = 64
WIDE = 2 * TILE
TOK = 512
FEAT = 672
PIECE = 84
PAD = 96
NSEM = 57
BLOCKS = ((0, 0), (0, 1), (1, 0), (3, 0), (1, 1), (3, 1), (2, 0), (2, 1))
ORDER_Z = (1, 7, 2, 6, 3, 5, 4)


def nt(a, b):
    return lax.dot_general(a, b, (((1,), (1,)), ((), ())), preferred_element_type=F32)


def tn(a, b):
    return lax.dot_general(a, b, (((0,), (0,)), ((), ())), preferred_element_type=F32)


def nn(a, b):
    return jnp.dot(a, b, preferred_element_type=F32)


def iotas(shape):
    return lax.broadcasted_iota(jnp.int32, shape, 0), lax.broadcasted_iota(jnp.int32, shape, 1)


def largest(a):
    return jnp.max(jnp.max(a, axis=1, keepdims=True), axis=0, keepdims=True)


def kernel(
    hidt, embt, tgt, pat, lgr, loss_o, hg_o, eg_o,
    hidp, piece, et, sbuf, sib, qout, qstep, qin, qin_step, lsum,
    gbuf, lbuf, xo, xin, pieces, pin, zsum, fin, ssem, rsem,
):
    x = lax.axis_index("dp")
    ctx = lax.axis_index("ctx")
    v = lax.axis_index("vocab")
    l, z = lax.div(ctx, NZ), lax.rem(ctx, NZ)
    h, c = lax.div(v, NC), lax.rem(v, NC)

    def dev(x, l, z, h, c):
        return (x, l * NZ + z, h * NC + c)

    def add(a, d, n):
        return lax.rem(a + d, n)

    sibling = dev(x, l, z, h, 1 - c)
    ring_h = [dev(x, l, z, add(h, dq, NH), c) for dq in range(NH)]
    xp, xm = dev(add(x, 1, NX), l, z, h, c), dev(add(x, 3, NX), l, z, h, c)
    yl = dev(x, 1 - l, z, h, c)
    ring_z = [dev(x, l, add(z, d, NZ), h, c) for d in range(NZ)]
    turned = dev(h, c, z, x, l)
    away, away_src = dev(h, c, z, x, 1 - l), dev(h, 1 - c, z, x, l)
    x2, h2 = add(x, 2, NX), add(h, 2, NX)
    far = [dev(x2, l, z, h, c), dev(x2, 1 - l, z, h, c)]
    far_away = [dev(h, c, z, x2, l), dev(h, c, z, x2, 1 - l)]
    far_away_src = [dev(h2, c, z, x, l), dev(h2, 1 - c, z, x, l)]
    diag = jnp.logical_and(x == h, l == c)
    off_diag = jnp.logical_not(diag)

    bar = pltpu.get_barrier_semaphore()

    def greet(who):
        pl.semaphore_signal(bar, inc=1, device_id=who, device_id_type=MESH)

    others = [(dq, dc) for dq in range(NH) for dc in range(NC) if dq or dc]
    others_dev = [dev(x, l, z, add(h, dq, NH), add(c, dc, NC)) for dq, dc in others]
    met = others_dev + [xp, xm, yl] + ring_z[1:] + far + far_away_src + [away_src]

    @pl.when(off_diag)
    def _():
        greet(turned)

    for who in met:
        greet(who)

    count = [0]
    sent = []

    def group():
        count[0] += 1
        return count[0] - 1

    def copy(src, dst, to, i):
        return pltpu.make_async_remote_copy(
            src_ref=src, dst_ref=dst, send_sem=ssem.at[i], recv_sem=rsem.at[i],
            device_id=to, device_id_type=MESH,
        )

    def wait_in(ref, i):
        copy(ref, ref, sibling, i).wait_recv()

    def wait_out(ref, i):
        copy(ref, ref, sibling, i).wait_send()

    def send_all(copies, ref):
        i = group()
        for src, dst, to in copies:
            copy(src, dst, to, i).start()
        sent.append((ref, i))
        return ref, i

    def send(src, dst, to):
        return send_all([(src, dst, to)], src)

    piece[...] = jnp.zeros((PAD, TILE), BF)
    piece[:PIECE] = embt[...]
    pl.semaphore_wait(bar, jnp.where(off_diag, len(met) + 1, len(met)))
    swap = copy(piece, et.at[0, z], turned, group())

    @pl.when(off_diag)
    def _():
        swap.start()

    @pl.when(diag)
    def _():
        et[0, z] = piece[...]

    hidp[...] = jnp.zeros((NZ, PAD, TOK), BF)
    for k in range(NZ):
        hidp[k, :PIECE] = hidt[k * PIECE : (k + 1) * PIECE]

    @pl.when(off_diag)
    def _():
        swap.wait()


    def index(d):
        return add(z, d, NZ)

    z_own = {d: send(et.at[0, z], et.at[0, z], ring_z[d]) for d in ORDER_Z}
    a1, groups = {}, [group() for _ in range(4)]

    def pass_on(src, dst, to, d, i):
        copy(et.at[src, index(d)], et.at[dst, index(d)], to, i).start()

    def spread_own(d):
        if d:
            wait_in(*z_own[NZ - d])
        part = et.at[0, index(d)]
        a1[d] = send(part, et.at[1, index(d)], yl)
        pass_on(0, 3, xp, d, groups[0])
        pass_on(0, 2, xm, d, groups[1])

    def spread_yl(d):
        wait_in(*a1[d])
        pass_on(1, 5, xp, d, groups[2])
        pass_on(1, 4, xm, d, groups[3])

    spread_own(0)
    far_in = [send(et.at[0, z], et.at[6 + m, z], far[m]) for m in range(2)]
    spread_own(1)
    spread_own(7)
    spread_yl(0)
    z_far = []
    for m in range(2):
        wait_in(*far_in[m])
        part = et.at[6 + m, z]
        copies = [(part, part, ring_z[d]) for d in ORDER_Z]
        z_far.append(send_all(copies, et.at[6 + m, pl.ds(0, NZ - 1)]))
    spread_own(2)
    spread_own(6)
    spread_yl(1)
    spread_yl(7)
    spread_own(3)
    spread_own(5)
    spread_yl(2)
    spread_yl(6)
    spread_own(4)
    spread_yl(3)
    spread_yl(5)
    spread_yl(4)
    for k, slot in enumerate((3, 2, 5, 4)):
        sent.append((et.at[slot], groups[k]))

    def weights(r):
        parts = [et[2 * r + m].reshape(NZ * PAD, TILE) for m in range(2)]
        return jnp.concatenate(parts, axis=1)

    def block_of(slot):
        dx, m = BLOCKS[slot]
        return 2 * add(x, dx, NX) + (1 - l if m else l)

    sib_cp, q_cp = {}, {}

    def logits(r):
        s = tn(hidp[...].reshape(NZ * PAD, TOK), weights(r))
        _, lane = iotas((TILE, WIDE))
        block = jnp.where(lane < TILE, block_of(2 * r), block_of(2 * r + 1))
        for t in range(NH):
            off = jnp.logical_and(block == v, pat[0:1, t : t + 1] == 0)
            part = jnp.where(off, DEAD, s[t * TILE : (t + 1) * TILE])
            sbuf[r, t] = part.reshape(NC, HALF, WIDE)
        sib_cp[r] = send(sbuf.at[r, :, 1 - c], sib.at[r], sibling)

    def mine(r, dq):
        t = add(h, dq, NH)
        return sbuf[r, t, c] + sib[r, t]

    def spread(r):
        wait_in(*sib_cp[r])
        tiles, steps = [], []
        for dq in (2, 1, 3):
            s = mine(r, dq)
            dead = s < 0.5 * DEAD
            peak = largest(jnp.where(dead, 0.0, jnp.abs(s)))
            step = jnp.maximum(peak, 1e-30) * (1.0 / TOP)
            near = jnp.clip(jnp.round(s * (1.0 / step)), -TOP, TOP)
            qout[r, dq - 1] = jnp.where(dead, -TOP - 1.0, near).astype(jnp.int32).astype(I16)
            qstep[r, dq - 1] = jnp.broadcast_to(step, (1, TILE))
            tiles.append((qout.at[r, dq - 1], qin.at[r, dq - 1], ring_h[dq]))
            steps.append((qstep.at[r, dq - 1], qin_step.at[r, dq - 1], ring_h[dq]))
        q_cp[r] = (send_all(steps, qstep.at[r]), send_all(tiles, qout.at[r]))

    def whole(r):
        total = mine(r, 0)
        for cp in q_cp[r]:
            wait_in(*cp)
        for k in range(NH - 1):
            steps = qin[r, k].astype(jnp.int32).astype(F32)
            total = total + jnp.where(steps < -TOP - 0.5, DEAD, steps * qin_step[r, k, 0:1, 0:1])
        lsum[r] = total

    logits(0)
    spread(0)
    wait_in(et.at[2], groups[1])
    wait_in(et.at[3], groups[0])
    logits(1)
    wait_in(et.at[4], groups[3])
    wait_in(et.at[5], groups[2])
    logits(2)
    spread(1)
    spread(2)
    for m in range(2):
        wait_in(*z_far[m])
    logits(3)
    whole(0)
    spread(3)
    whole(1)
    whole(2)
    whole(3)

    sub, lane = iotas((HALF, TILE))
    turn = sub + c * HALF == lane

    def column(row):
        return jnp.sum(jnp.where(turn, row, 0.0), axis=1, keepdims=True)

    target = column(tgt[pl.ds(h, 1), :].astype(F32)).astype(jnp.int32)
    scale = column(lgr[pl.ds(h, 1), :])
    _, lane2 = iotas((HALF, WIDE))
    hits, ls = [], []
    for r in range(NX):
        col = jnp.where(lane2 < TILE, block_of(2 * r), block_of(2 * r + 1) - 1) * TILE + lane2
        hits.append(col == target)
        ls.append(lsum[r])
    peak = jnp.maximum(jnp.maximum(ls[0], ls[1]), jnp.maximum(ls[2], ls[3]))
    peak = jnp.max(peak, axis=1, keepdims=True)
    total = jnp.sum(sum(jnp.exp(s - peak) for s in ls), axis=1, keepdims=True)
    lse = peak + jnp.log(total)
    at_target = sum(jnp.where(hit, s, 0.0) for hit, s in zip(hits, ls))
    loss = lse - jnp.sum(at_target, axis=1, keepdims=True)
    g_cp, relay = {}, {}
    for r in (3, 1, 2, 0):
        probs = jnp.exp(ls[r] - lse)
        gbuf[r, h, c] = (scale * (probs - jnp.where(hits[r], 1.0, 0.0))).astype(BF)
        own = gbuf.at[r, h, c]
        copies = [(own, own, ring_h[dq]) for dq in (2, 1, 3)]
        g_cp[r] = send_all(copies, gbuf.at[r, pl.ds(0, NH - 1), 0])
    lbuf[v] = jnp.sum(jnp.where(turn, loss, 0.0), axis=0, keepdims=True)
    copies = [(lbuf.at[v], lbuf.at[v], who) for who in others_dev]
    loss_cp = send_all(copies, lbuf.at[pl.ds(0, NH * NC - 1)])

    def pair(r):
        wait_in(*g_cp[r])
        part = gbuf.at[r, :, c]
        relay[r] = send(part, part, sibling)

    def grad(r):
        wait_in(*relay[r])
        return nn(hidt[...], gbuf[r].reshape(TOK, WIDE))

    def to_near(m):
        d = grad(1 + m)
        out = []
        for side, to in enumerate((xp, xm)):
            xo[side, m] = d[:, side * TILE : (side + 1) * TILE].astype(BF)
            out.append(send(xo.at[side, m], xin.at[side, m], to))
        return out

    def to_z(slot, tot):
        for k in range(NZ):
            pieces[slot, k, :PIECE] = tot[k * PIECE : (k + 1) * PIECE].astype(BF)
        pin[slot, z] = pieces[slot, z]
        copies = [(pieces.at[slot, index(d)], pin.at[slot, z], ring_z[d]) for d in ORDER_Z]
        return send_all(copies, pieces.at[slot, pl.ds(0, NZ - 1)])

    def sum_z(slot):
        wait_in(*z_cp[slot])
        total = pin[slot, 0].astype(F32)
        for k in range(1, NZ):
            total = total + pin[slot, k].astype(F32)
        zsum[slot] = total.astype(BF)

    pieces[...] = jnp.zeros((4, NZ, PAD, TILE), BF)
    pair(3)
    d = grad(3)
    z_cp = {2 + m: to_z(2 + m, d[:, m * TILE : (m + 1) * TILE]) for m in range(2)}
    pair(1)
    near = [to_near(0)]
    pair(2)
    near.append(to_near(1))
    pair(0)
    own = grad(0)
    for m in range(2):
        for cp in near[m]:
            wait_in(*cp)
        both = xin[0, m].astype(F32) + xin[1, m].astype(F32)
        z_cp[m] = to_z(m, own[:, m * TILE : (m + 1) * TILE] + both)

    hg = nt(weights(0), gbuf[0].reshape(TOK, WIDE))
    for r in range(1, NX):
        hg = hg + nt(weights(r), gbuf[r].reshape(TOK, WIDE))
    for k in range(NZ):
        hg_o[k * PIECE : (k + 1) * PIECE] = hg[k * PAD : k * PAD + PIECE].astype(BF)
    wait_in(*loss_cp)
    for t in range(NH):
        loss_o[t : t + 1, :] = lbuf[2 * t] + lbuf[2 * t + 1]

    end = []
    for slot in (2, 3):
        sum_z(slot)
        end.append(send(zsum.at[slot], fin.at[slot], far_away[slot - 2]))
    sum_z(0)
    end0 = copy(zsum.at[0], fin.at[0], turned, group())

    @pl.when(off_diag)
    def _():
        end0.start()

    @pl.when(diag)
    def _():
        fin[0] = zsum[0]

    sum_z(1)
    end.append(send(zsum.at[1], fin.at[1], away))
    for cp in end:
        wait_in(*cp)

    @pl.when(off_diag)
    def _():
        end0.wait()

    total = fin[0].astype(F32)
    for slot in range(1, 4):
        total = total + fin[slot].astype(F32)
    eg_o[...] = total[:PIECE]
    for cp in sent:
        wait_out(*cp)


def on_device(hidden, embedding, targets, pattern, loss_grad):
    vmem = pl.BlockSpec(memory_space=pltpu.VMEM)
    loss, hidden_grad, embedding_grad = pl.pallas_call(
        kernel,
        out_shape=(
            jax.ShapeDtypeStruct((NH, TILE), F32),
            jax.ShapeDtypeStruct((FEAT, TOK), BF),
            jax.ShapeDtypeStruct((PIECE, TILE), F32),
        ),
        in_specs=[vmem] * 5,
        out_specs=(vmem,) * 3,
        scratch_shapes=[
            pltpu.VMEM((NZ, PAD, TOK), BF),
            pltpu.VMEM((PAD, TILE), BF),
            pltpu.VMEM((8, NZ, PAD, TILE), BF),
            pltpu.VMEM((NX, NH, NC, HALF, WIDE), F32),
            pltpu.VMEM((NX, NH, HALF, WIDE), F32),
            pltpu.VMEM((NX, NH - 1, HALF, WIDE), I16),
            pltpu.VMEM((NX, NH - 1, 1, TILE), F32),
            pltpu.VMEM((NX, NH - 1, HALF, WIDE), I16),
            pltpu.VMEM((NX, NH - 1, 1, TILE), F32),
            pltpu.VMEM((NX, HALF, WIDE), F32),
            pltpu.VMEM((NX, NH, NC, HALF, WIDE), BF),
            pltpu.VMEM((NH * NC, 1, TILE), F32),
            pltpu.VMEM((2, 2, FEAT, TILE), BF),
            pltpu.VMEM((2, 2, FEAT, TILE), BF),
            pltpu.VMEM((4, NZ, PAD, TILE), BF),
            pltpu.VMEM((4, NZ, PAD, TILE), BF),
            pltpu.VMEM((4, PAD, TILE), BF),
            pltpu.VMEM((4, PAD, TILE), BF),
            pltpu.SemaphoreType.DMA((NSEM,)),
            pltpu.SemaphoreType.DMA((NSEM,)),
        ],
        compiler_params=pltpu.CompilerParams(
            collective_id=0, has_side_effects=True, vmem_limit_bytes=48 << 20
        ),
    )(hidden.T, embedding.T, targets.reshape(NH, TILE), pattern.T, loss_grad.reshape(NH, TILE))
    return loss.reshape(TOK), hidden_grad.T, embedding_grad.T


def solution(mesh):
    return jax.shard_map(
        on_device,
        mesh=mesh,
        in_specs=(
            P(("dp", "ctx"), "vocab"),
            P("vocab", ("dp", "ctx")),
            P(("dp", "ctx")),
            P(("dp", "ctx"), "vocab"),
            P(("dp", "ctx")),
        ),
        out_specs=(P(("dp", "ctx")), P(("dp", "ctx"), "vocab"), P("vocab", ("dp", "ctx"))),
        check_vma=False,
    )
```

```python
import jax
import jax.numpy as jnp
from jax import lax
from jax.experimental import pallas as pl
from jax.experimental.pallas import tpu as pltpu
from jax.sharding import PartitionSpec as P

MESH = pl.DeviceIdType.MESH
BF = jnp.bfloat16
F32 = jnp.float32
I16 = jnp.int16
DEAD = -1e30
TOP = 32767.0
NX, NL, NZ, NH, NC = 4, 2, 8, 4, 2
TILE = 128
HALF = 64
WIDE = 2 * TILE
TOK = 512
FEAT = 672
PIECE = 84
PAD = 96
NSEM = 57
BLOCKS = ((0, 0), (0, 1), (1, 0), (3, 0), (1, 1), (3, 1), (2, 0), (2, 1))
ORDER_Z = (1, 7, 2, 6, 3, 5, 4)


def nt(a, b):
    return lax.dot_general(a, b, (((1,), (1,)), ((), ())), preferred_element_type=F32)


def tn(a, b):
    return lax.dot_general(a, b, (((0,), (0,)), ((), ())), preferred_element_type=F32)


def nn(a, b):
    return jnp.dot(a, b, preferred_element_type=F32)


def iotas(shape):
    return lax.broadcasted_iota(jnp.int32, shape, 0), lax.broadcasted_iota(jnp.int32, shape, 1)


def largest(a):
    return jnp.max(jnp.max(a, axis=1, keepdims=True), axis=0, keepdims=True)


def kernel(
    hidt, embt, tgt, pat, lgr, loss_o, hg_o, eg_o,
    hidp, piece, et, sbuf, sib, qout, qstep, qin, qin_step, lsum,
    gbuf, lbuf, xo, xin, xfar, xfar_in, pieces, pin, zsum, fin, ssem, rsem,
):
    x = lax.axis_index("dp")
    ctx = lax.axis_index("ctx")
    v = lax.axis_index("vocab")
    l, z = lax.div(ctx, NZ), lax.rem(ctx, NZ)
    h, c = lax.div(v, NC), lax.rem(v, NC)

    def dev(x, l, z, h, c):
        return (x, l * NZ + z, h * NC + c)

    def add(a, d, n):
        return lax.rem(a + d, n)

    sibling = dev(x, l, z, h, 1 - c)
    ring_h = [dev(x, l, z, add(h, dq, NH), c) for dq in range(NH)]
    xp, xm = dev(add(x, 1, NX), l, z, h, c), dev(add(x, 3, NX), l, z, h, c)
    yl = dev(x, 1 - l, z, h, c)
    ring_z = [dev(x, l, add(z, d, NZ), h, c) for d in range(NZ)]
    turned = dev(h, c, z, x, l)
    away, away_src = dev(h, c, z, x, 1 - l), dev(h, 1 - c, z, x, l)
    x2, h2 = add(x, 2, NX), add(h, 2, NX)
    far = [dev(x2, l, z, h, c), dev(x2, 1 - l, z, h, c)]
    far_away, far_away_src = dev(h, c, z, x2, l), dev(h2, c, z, x, l)
    diag = jnp.logical_and(x == h, l == c)
    off_diag = jnp.logical_not(diag)

    bar = pltpu.get_barrier_semaphore()

    def greet(who):
        pl.semaphore_signal(bar, inc=1, device_id=who, device_id_type=MESH)

    others = [(dq, dc) for dq in range(NH) for dc in range(NC) if dq or dc]
    others_dev = [dev(x, l, z, add(h, dq, NH), add(c, dc, NC)) for dq, dc in others]
    met = others_dev + [xp, xm, yl] + ring_z[1:] + far + [far_away_src, away_src]

    @pl.when(off_diag)
    def _():
        greet(turned)

    for who in met:
        greet(who)

    count = [0]
    sent = []

    def group():
        count[0] += 1
        return count[0] - 1

    def copy(src, dst, to, i):
        return pltpu.make_async_remote_copy(
            src_ref=src, dst_ref=dst, send_sem=ssem.at[i], recv_sem=rsem.at[i],
            device_id=to, device_id_type=MESH,
        )

    def wait_in(ref, i):
        copy(ref, ref, sibling, i).wait_recv()

    def wait_out(ref, i):
        copy(ref, ref, sibling, i).wait_send()

    def send_all(copies, ref):
        i = group()
        for src, dst, to in copies:
            copy(src, dst, to, i).start()
        sent.append((ref, i))
        return ref, i

    def send(src, dst, to):
        return send_all([(src, dst, to)], src)

    piece[...] = jnp.zeros((PAD, TILE), BF)
    piece[:PIECE] = embt[...]
    pl.semaphore_wait(bar, jnp.where(off_diag, len(met) + 1, len(met)))
    swap = copy(piece, et.at[0, z], turned, group())

    @pl.when(off_diag)
    def _():
        swap.start()

    @pl.when(diag)
    def _():
        et[0, z] = piece[...]

    hidp[...] = jnp.zeros((NZ, PAD, TOK), BF)
    for k in range(NZ):
        hidp[k, :PIECE] = hidt[k * PIECE : (k + 1) * PIECE]

    @pl.when(off_diag)
    def _():
        swap.wait()


    def index(d):
        return add(z, d, NZ)

    z_own = {d: send(et.at[0, z], et.at[0, z], ring_z[d]) for d in ORDER_Z}
    a1, groups = {}, [group() for _ in range(4)]

    def pass_on(src, dst, to, d, i):
        copy(et.at[src, index(d)], et.at[dst, index(d)], to, i).start()

    def spread_own(d):
        if d:
            wait_in(*z_own[NZ - d])
        part = et.at[0, index(d)]
        a1[d] = send(part, et.at[1, index(d)], yl)
        pass_on(0, 3, xp, d, groups[0])
        pass_on(0, 2, xm, d, groups[1])

    def spread_yl(d):
        wait_in(*a1[d])
        pass_on(1, 5, xp, d, groups[2])
        pass_on(1, 4, xm, d, groups[3])

    spread_own(0)
    far_in = [send(et.at[0, z], et.at[6 + m, z], far[m]) for m in range(2)]
    spread_own(1)
    spread_own(7)
    spread_yl(0)
    z_far = []
    for m in range(2):
        wait_in(*far_in[m])
        part = et.at[6 + m, z]
        copies = [(part, part, ring_z[d]) for d in ORDER_Z]
        z_far.append(send_all(copies, et.at[6 + m, pl.ds(0, NZ - 1)]))
    spread_own(2)
    spread_own(6)
    spread_yl(1)
    spread_yl(7)
    spread_own(3)
    spread_own(5)
    spread_yl(2)
    spread_yl(6)
    spread_own(4)
    spread_yl(3)
    spread_yl(5)
    spread_yl(4)
    for k, slot in enumerate((3, 2, 5, 4)):
        sent.append((et.at[slot], groups[k]))

    def weights(r):
        parts = [et[2 * r + m].reshape(NZ * PAD, TILE) for m in range(2)]
        return jnp.concatenate(parts, axis=1)

    def block_of(slot):
        dx, m = BLOCKS[slot]
        return 2 * add(x, dx, NX) + (1 - l if m else l)

    sib_cp, q_cp = {}, {}

    def logits(r):
        s = tn(hidp[...].reshape(NZ * PAD, TOK), weights(r))
        _, lane = iotas((TILE, WIDE))
        block = jnp.where(lane < TILE, block_of(2 * r), block_of(2 * r + 1))
        for t in range(NH):
            off = jnp.logical_and(block == v, pat[0:1, t : t + 1] == 0)
            part = jnp.where(off, DEAD, s[t * TILE : (t + 1) * TILE])
            sbuf[r, t] = part.reshape(NC, HALF, WIDE)
        sib_cp[r] = send(sbuf.at[r, :, 1 - c], sib.at[r], sibling)

    def mine(r, dq):
        t = add(h, dq, NH)
        return sbuf[r, t, c] + sib[r, t]

    def spread(r):
        wait_in(*sib_cp[r])
        tiles, steps = [], []
        for dq in (2, 1, 3):
            s = mine(r, dq)
            dead = s < 0.5 * DEAD
            peak = largest(jnp.where(dead, 0.0, jnp.abs(s)))
            step = jnp.maximum(peak, 1e-30) * (1.0 / TOP)
            near = jnp.clip(jnp.round(s * (1.0 / step)), -TOP, TOP)
            qout[r, dq - 1] = jnp.where(dead, -TOP - 1.0, near).astype(jnp.int32).astype(I16)
            qstep[r, dq - 1] = jnp.broadcast_to(step, (1, TILE))
            tiles.append((qout.at[r, dq - 1], qin.at[r, dq - 1], ring_h[dq]))
            steps.append((qstep.at[r, dq - 1], qin_step.at[r, dq - 1], ring_h[dq]))
        q_cp[r] = (send_all(steps, qstep.at[r]), send_all(tiles, qout.at[r]))

    def whole(r):
        total = mine(r, 0)
        for cp in q_cp[r]:
            wait_in(*cp)
        for k in range(NH - 1):
            steps = qin[r, k].astype(jnp.int32).astype(F32)
            total = total + jnp.where(steps < -TOP - 0.5, DEAD, steps * qin_step[r, k, 0:1, 0:1])
        lsum[r] = total

    logits(0)
    spread(0)
    wait_in(et.at[2], groups[1])
    wait_in(et.at[3], groups[0])
    logits(1)
    wait_in(et.at[4], groups[3])
    wait_in(et.at[5], groups[2])
    logits(2)
    spread(1)
    spread(2)
    for m in range(2):
        wait_in(*z_far[m])
    logits(3)
    whole(0)
    spread(3)
    whole(1)
    whole(2)
    whole(3)

    sub, lane = iotas((HALF, TILE))
    turn = sub + c * HALF == lane

    def column(row):
        return jnp.sum(jnp.where(turn, row, 0.0), axis=1, keepdims=True)

    target = column(tgt[pl.ds(h, 1), :].astype(F32)).astype(jnp.int32)
    scale = column(lgr[pl.ds(h, 1), :])
    _, lane2 = iotas((HALF, WIDE))
    hits, ls = [], []
    for r in range(NX):
        col = jnp.where(lane2 < TILE, block_of(2 * r), block_of(2 * r + 1) - 1) * TILE + lane2
        hits.append(col == target)
        ls.append(lsum[r])
    peak = jnp.maximum(jnp.maximum(ls[0], ls[1]), jnp.maximum(ls[2], ls[3]))
    peak = jnp.max(peak, axis=1, keepdims=True)
    total = jnp.sum(sum(jnp.exp(s - peak) for s in ls), axis=1, keepdims=True)
    lse = peak + jnp.log(total)
    at_target = sum(jnp.where(hit, s, 0.0) for hit, s in zip(hits, ls))
    loss = lse - jnp.sum(at_target, axis=1, keepdims=True)
    g_cp, relay = {}, {}
    for r in (3, 1, 2, 0):
        probs = jnp.exp(ls[r] - lse)
        gbuf[r, h, c] = (scale * (probs - jnp.where(hits[r], 1.0, 0.0))).astype(BF)
        own = gbuf.at[r, h, c]
        copies = [(own, own, ring_h[dq]) for dq in (2, 1, 3)]
        g_cp[r] = send_all(copies, gbuf.at[r, pl.ds(0, NH - 1), 0])
    lbuf[v] = jnp.sum(jnp.where(turn, loss, 0.0), axis=0, keepdims=True)
    copies = [(lbuf.at[v], lbuf.at[v], who) for who in others_dev]
    loss_cp = send_all(copies, lbuf.at[pl.ds(0, NH * NC - 1)])

    def pair(r):
        wait_in(*g_cp[r])
        part = gbuf.at[r, :, c]
        relay[r] = send(part, part, sibling)

    def grad(r):
        wait_in(*relay[r])
        return nn(hidt[...], gbuf[r].reshape(TOK, WIDE))

    def to_near(m):
        d = grad(1 + m)
        out = []
        for side, to in enumerate((xp, xm)):
            part = d[:, side * TILE : (side + 1) * TILE]
            if m:
                wait_in(*far_x[side])
                passing = xfar_in[side].astype(F32)
                halves = [part[: FEAT // 2], part[FEAT // 2 :]]
                halves[side] = halves[side] + passing
                part = jnp.concatenate(halves, axis=0)
            xo[side, m] = part.astype(BF)
            out.append(send(xo.at[side, m], xin.at[side, m], to))
        return out

    def to_z(slot, tot):
        for k in range(NZ):
            pieces[slot, k, :PIECE] = tot[k * PIECE : (k + 1) * PIECE].astype(BF)
        pin[slot, z] = pieces[slot, z]
        copies = [(pieces.at[slot, index(d)], pin.at[slot, z], ring_z[d]) for d in (4, 3, 5, 2, 6, 1, 7)]
        return send_all(copies, pieces.at[slot, pl.ds(0, NZ - 1)])

    def sum_z(slot):
        wait_in(*z_cp[slot])
        total = pin[slot, 0].astype(F32)
        for k in range(1, NZ):
            total = total + pin[slot, k].astype(F32)
        zsum[slot] = total.astype(BF)

    pieces[...] = jnp.zeros((4, NZ, PAD, TILE), BF)
    pair(3)
    d = grad(3)
    far_x = []
    for side, to in enumerate((xp, xm)):
        rows = slice(side * FEAT // 2, (side + 1) * FEAT // 2)
        xfar[side] = d[rows, TILE:].astype(BF)
        far_x.append(send(xfar.at[side], xfar_in.at[side], to))
    z_cp = {2: to_z(2, d[:, :TILE])}
    pair(1)
    near = [to_near(0)]
    pair(2)
    near.append(to_near(1))
    pair(0)
    own = grad(0)
    for m in range(2):
        for cp in near[m]:
            wait_in(*cp)
        both = xin[0, m].astype(F32) + xin[1, m].astype(F32)
        z_cp[m] = to_z(m, own[:, m * TILE : (m + 1) * TILE] + both)

    hg = nt(weights(0), gbuf[0].reshape(TOK, WIDE))
    for r in range(1, NX):
        hg = hg + nt(weights(r), gbuf[r].reshape(TOK, WIDE))
    for k in range(NZ):
        hg_o[k * PIECE : (k + 1) * PIECE] = hg[k * PAD : k * PAD + PIECE].astype(BF)
    wait_in(*loss_cp)
    for t in range(NH):
        loss_o[t : t + 1, :] = lbuf[2 * t] + lbuf[2 * t + 1]

    end = []
    sum_z(2)
    end.append(send(zsum.at[2], fin.at[2], far_away))
    sum_z(0)
    end0 = copy(zsum.at[0], fin.at[0], turned, group())

    @pl.when(off_diag)
    def _():
        end0.start()

    @pl.when(diag)
    def _():
        fin[0] = zsum[0]

    sum_z(1)
    end.append(send(zsum.at[1], fin.at[1], away))
    for cp in end:
        wait_in(*cp)

    @pl.when(off_diag)
    def _():
        end0.wait()

    total = fin[0].astype(F32)
    for slot in range(1, 3):
        total = total + fin[slot].astype(F32)
    eg_o[...] = total[:PIECE]
    for cp in sent:
        wait_out(*cp)


def on_device(hidden, embedding, targets, pattern, loss_grad):
    vmem = pl.BlockSpec(memory_space=pltpu.VMEM)
    loss, hidden_grad, embedding_grad = pl.pallas_call(
        kernel,
        out_shape=(
            jax.ShapeDtypeStruct((NH, TILE), F32),
            jax.ShapeDtypeStruct((FEAT, TOK), BF),
            jax.ShapeDtypeStruct((PIECE, TILE), F32),
        ),
        in_specs=[vmem] * 5,
        out_specs=(vmem,) * 3,
        scratch_shapes=[
            pltpu.VMEM((NZ, PAD, TOK), BF),
            pltpu.VMEM((PAD, TILE), BF),
            pltpu.VMEM((8, NZ, PAD, TILE), BF),
            pltpu.VMEM((NX, NH, NC, HALF, WIDE), F32),
            pltpu.VMEM((NX, NH, HALF, WIDE), F32),
            pltpu.VMEM((NX, NH - 1, HALF, WIDE), I16),
            pltpu.VMEM((NX, NH - 1, 1, TILE), F32),
            pltpu.VMEM((NX, NH - 1, HALF, WIDE), I16),
            pltpu.VMEM((NX, NH - 1, 1, TILE), F32),
            pltpu.VMEM((NX, HALF, WIDE), F32),
            pltpu.VMEM((NX, NH, NC, HALF, WIDE), BF),
            pltpu.VMEM((NH * NC, 1, TILE), F32),
            pltpu.VMEM((2, 2, FEAT, TILE), BF),
            pltpu.VMEM((2, 2, FEAT, TILE), BF),
            pltpu.VMEM((2, FEAT // 2, TILE), BF),
            pltpu.VMEM((2, FEAT // 2, TILE), BF),
            pltpu.VMEM((4, NZ, PAD, TILE), BF),
            pltpu.VMEM((4, NZ, PAD, TILE), BF),
            pltpu.VMEM((4, PAD, TILE), BF),
            pltpu.VMEM((4, PAD, TILE), BF),
            pltpu.SemaphoreType.DMA((NSEM,)),
            pltpu.SemaphoreType.DMA((NSEM,)),
        ],
        compiler_params=pltpu.CompilerParams(
            collective_id=0, has_side_effects=True, vmem_limit_bytes=48 << 20
        ),
    )(hidden.T, embedding.T, targets.reshape(NH, TILE), pattern.T, loss_grad.reshape(NH, TILE))
    return loss.reshape(TOK), hidden_grad.T, embedding_grad.T


def solution(mesh):
    return jax.shard_map(
        on_device,
        mesh=mesh,
        in_specs=(
            P(("dp", "ctx"), "vocab"),
            P("vocab", ("dp", "ctx")),
            P(("dp", "ctx")),
            P(("dp", "ctx"), "vocab"),
            P(("dp", "ctx")),
        ),
        out_specs=(P(("dp", "ctx")), P(("dp", "ctx"), "vocab"), P("vocab", ("dp", "ctx"))),
        check_vma=False,
    )
```
